32 devices in a mesh: dp: 8 (over z, x), seq: 4 (over y, core).
Axes of the slice: x: 2, y: 2, z: 4, core: 2. Of those that a mesh axis runs over, the one named last changes fastest.
Arguments:
- tokens: bfloat16 [8, 4096, 768], P('dp', 'seq'), may hold values from -6 to 6
- lengths: int32 [8], P('dp'), may hold values from 512 to 4096, as said below
- cotangent: bfloat16 [8, 4096, 768], P('dp', 'seq'), may hold values from -6 to 6
- norm_gain: float32 [768], replicated, may hold values from 0.5 to 1.5
- w_z: bfloat16 [768, 1536], replicated, may hold values from -0.21875 to 0.21875
- w_xbc: bfloat16 [768, 1792], replicated, may hold values from -0.21875 to 0.21875
- w_dt: bfloat16 [768, 24], replicated, may hold values from -0.21875 to 0.21875
- conv_weight: float32 [4, 1792], replicated, may hold values from -0.5 to 0.5
- conv_bias: float32 [1792], replicated, may hold values from -0.5 to 0.5
- dt_bias: float32 [24], replicated, may hold values from -6 to -3
- a_log: float32 [24], replicated, may hold values from -2.5 to 1
- d_skip: float32 [24], replicated, may hold values from 0.5 to 1.5
- gate_gain: float32 [1536], replicated, may hold values from 0.5 to 1.5
- w_out: bfloat16 [1536, 768], replicated, may hold values from -0.15625 to 0.15625
Outputs:
- block_out: bfloat16 [8, 4096, 768], P('dp', 'seq')
- input_grad: bfloat16 [8, 4096, 768], P('dp', 'seq')
- grad_norm_gain: float32 [768], replicated
- grad_w_z: float32 [768, 1536], replicated
- grad_w_xbc: float32 [768, 1792], replicated
- grad_w_dt: float32 [768, 24], replicated
- grad_conv_weight: float32 [4, 1792], replicated
- grad_conv_bias: float32 [1792], replicated
- grad_dt_bias: float32 [24], replicated
- grad_a_log: float32 [24], replicated
- grad_d_skip: float32 [24], replicated
- grad_gate_gain: float32 [1536], replicated
- grad_w_out: float32 [1536, 768], replicated
The draws below stay inside these ranges and needn't reach their ends.
Inputs may be any that keep to these rules, and one draw needn't show every extreme that they name: lengths[b] counts the real positions of sequence b, which fill positions 0 to lengths[b] - 1 of its row; the rest is padding. In every draw some sequence fills all 4096 positions.
All inputs are finite; a program needn't handle non-finite values.
Results may differ from the reference program's by a relative error of at most 0.012.
The reference program's roundings to bfloat16 on the way count: a program that leaves them out, or rounds other values in their place, can miss the bound.
Values may be sent and summed in bfloat16 or wider, within the bound.
A program may use at most 192 MiB of HBM per device.

```python
from functools import partial
import jax
import jax.numpy as jnp
from jax import lax

D = 768
HEADS = 24
HEAD_DIM = 64
STATE = 128
CONV = 4
GROUP = 256
INNER = 1536
XBC = 1792
ROW = 4096
BATCH = 8


def draw_lengths(key, part):
    key = jax.random.fold_in(key, 7)
    level_key, offset_key, fill_key = jax.random.split(key, 3)
    lowest = ROW // 8
    levels = jax.random.randint(level_key, (BATCH,), 0, 3)
    starts = jnp.left_shift(jnp.full((BATCH,), lowest, jnp.int32), levels.astype(jnp.int32))
    offsets = jax.random.randint(offset_key, (BATCH,), 0, starts)
    drawn = starts + offsets
    filled = jax.random.randint(fill_key, (), 0, BATCH)
    return jnp.where(jnp.arange(BATCH) == filled, ROW, drawn).astype(jnp.int32)


def steps_of(stream_key, dims, cuts, low, high):
    factor_of, own = 1.0, jax.random.fold_in(stream_key, 6)
    for dim, parts in cuts:
        heights = jnp.exp(jax.random.uniform(jax.random.fold_in(own, dim), (parts,), jnp.float32, low / len(cuts), high / len(cuts)))
        factor_of = factor_of * jnp.repeat(heights, dims[dim] // parts).reshape([-1 if axis == dim else 1 for axis in range(len(dims))])
    return factor_of


def scatter_about(stream_key, extent, scale, reach, pieces=(), kind=jnp.bfloat16):
    values = jax.random.normal(stream_key, extent, jnp.float32) * scale
    if len(pieces) > 0:
        values = steps_of(stream_key, extent, pieces, -0.22, 0.18) * values
    return jnp.clip(values, min=-reach, max=reach).astype(kind)


def setup_inputs(seed: int = 0) -> dict:
    key_of = jax.random.split(jax.random.key(seed), 15)
    return {
        "tokens": scatter_about(key_of[0], (BATCH, ROW, D), 1.0, 6.0, ((0, 8), (1, 4))),
        "lengths": draw_lengths(jax.random.fold_in(key_of[14], 71), 0),
        "cotangent": scatter_about(key_of[2], (BATCH, ROW, D), 1.0, 6.0, ((0, 8), (1, 4))),
        "norm_gain": jnp.clip(1.0 + 0.1 * jax.random.normal(key_of[3], (D,), jnp.float32), 0.5, 1.5),
        "w_z": scatter_about(key_of[4], (D, INNER), D ** -0.5, 0.21875),
        "w_xbc": scatter_about(key_of[5], (D, XBC), D ** -0.5, 0.21875),
        "w_dt": scatter_about(key_of[6], (D, HEADS), D ** -0.5, 0.21875),
        "conv_weight": jnp.clip(jax.random.uniform(key_of[7], (CONV, XBC), jnp.float32, -0.5, 0.5), -0.5, 0.5),
        "conv_bias": jnp.clip(jax.random.uniform(key_of[8], (XBC,), jnp.float32, -0.5, 0.5), -0.5, 0.5),
        "dt_bias": jnp.clip(jax.random.uniform(key_of[9], (HEADS,), jnp.float32, -6.0, -3.0), -6.0, -3.0),
        "a_log": jnp.clip(jax.random.uniform(key_of[10], (HEADS,), jnp.float32, -2.5, 1.0), -2.5, 1.0),
        "d_skip": jnp.clip(jax.random.uniform(key_of[11], (HEADS,), jnp.float32, 0.5, 1.5), 0.5, 1.5),
        "gate_gain": jnp.clip(1.0 + 0.1 * jax.random.normal(key_of[12], (INNER,), jnp.float32), 0.5, 1.5),
        "w_out": scatter_about(key_of[13], (INNER, D), INNER ** -0.5, 0.15625),
    }


EPSILON = 1e-05
HIGH = lax.Precision.HIGHEST

@jax.custom_vjp
def low(v):
    return lax.optimization_barrier(v.astype(jnp.bfloat16)).astype(jnp.float32)

@jax.custom_vjp
def low_back(v):
    return v

def low_keep(v):
    return (low(v), None)

def low_pass(kept, grad):
    return (grad,)

def back_keep(v):
    return (v, None)

def back_low(kept, grad):
    return (low(grad),)
low.defvjp(low_keep, low_pass)
low_back.defvjp(back_keep, back_low)

def matmul_hi(left, right):
    return jnp.dot(left, right, precision=HIGH, preferred_element_type=jnp.float32)

def state_scan(values, steps_dt, rates, b_mat, c_mat):
    total_rows, heads_here, width = values.shape
    group_count = total_rows // GROUP
    state_width = b_mat.shape[1]
    inflow = (steps_dt[:, :, None] * values).reshape(group_count, GROUP, heads_here, width)
    log_rates = jnp.swapaxes((steps_dt * rates[None, :]).reshape(group_count, GROUP, heads_here), 1, 2)
    running = jnp.cumsum(log_rates, axis=2)
    causal = jnp.arange(GROUP)[:, None] >= jnp.arange(GROUP)[None, :]
    decays = jnp.exp(jnp.where(causal, running[:, :, :, None] - running[:, :, None, :], -1e+30))
    b_groups = b_mat.reshape(group_count, GROUP, state_width)
    c_groups = c_mat.reshape(group_count, GROUP, state_width)
    intersections = jnp.einsum('ctn,csn->cts', c_groups, b_groups, precision=HIGH)
    scores = decays * intersections[:, None, :, :]
    within = jnp.einsum('chts,cshp->cthp', scores, inflow, precision=HIGH)
    final_log = running[:, :, -1]
    to_end = jnp.exp(final_log[:, :, None] - running)
    weighted = inflow * jnp.swapaxes(to_end, 1, 2)[:, :, :, None]
    group_state = jnp.einsum('csn,cshp->chpn', b_groups, weighted, precision=HIGH)

    def advance(state_in, carried_item):
        factor, added = carried_item
        return (factor[:, None, None] * state_in + added, state_in)
    zero_state = jnp.zeros((heads_here, width, state_width), jnp.float32)
    unused, starts = lax.scan(advance, zero_state, (jnp.exp(final_log), group_state))
    carried = jnp.einsum('ctn,chpn->cthp', c_groups, starts, precision=HIGH)
    carried = carried * jnp.swapaxes(jnp.exp(running), 1, 2)[:, :, :, None]
    return (within + carried).reshape(total_rows, heads_here, width)

def branch_row(weights, block_in, length):
    norm_gain, w_z, w_xbc, w_dt, conv_weight, conv_bias, dt_bias, a_log, d_skip, gate_gain, w_out = weights
    rms = lax.rsqrt(lax.optimization_barrier(jnp.mean(block_in * block_in, axis=-1, keepdims=True)) + EPSILON)
    normed = low(block_in * rms * norm_gain)
    gate_pre = low_back(matmul_hi(normed, w_z))
    xbc = low(low_back(matmul_hi(normed, w_xbc)))
    dt_raw = low_back(matmul_hi(normed, w_dt))
    padded = jnp.concatenate([jnp.zeros((CONV - 1, XBC), jnp.float32), xbc], axis=0)
    conv_out = conv_bias[None, :] + conv_weight[0][None, :] * padded[0:ROW]
    for offset in range(1, CONV):
        conv_out = conv_out + conv_weight[offset][None, :] * padded[offset:offset + ROW]
    act = jax.nn.silu(conv_out)
    x_heads = low(low_back(act[:, :INNER])).reshape(ROW, HEADS, HEAD_DIM)
    b_and_c = low(act[:, INNER:])
    dt_value = low(low_back(jax.nn.softplus(dt_raw + dt_bias[None, :])))
    rates = -jnp.exp(a_log)
    scanned = state_scan(x_heads, dt_value, rates, b_and_c[:, :STATE], b_and_c[:, STATE:])
    y_value = scanned + d_skip[None, :, None] * x_heads
    y_value = low(low_back(y_value.reshape(ROW, INNER)))
    gated = y_value * jax.nn.silu(gate_pre)
    rms_gate = lax.rsqrt(lax.optimization_barrier(jnp.mean(gated * gated, axis=-1, keepdims=True)) + EPSILON)
    o_value = low(gated * rms_gate * gate_gain[None, :])
    branch = matmul_hi(o_value, w_out)
    live = jnp.arange(ROW, dtype=jnp.int32) < length
    return block_in + jnp.where(live[:, None], branch, 0.0)

def reference(tokens, lengths, cotangent, norm_gain, w_z, w_xbc, w_dt, conv_weight, conv_bias, dt_bias, a_log, d_skip, gate_gain, w_out):
    weights = (norm_gain.astype(jnp.float32), w_z.astype(jnp.float32), w_xbc.astype(jnp.float32), w_dt.astype(jnp.float32), conv_weight.astype(jnp.float32), conv_bias.astype(jnp.float32), dt_bias.astype(jnp.float32), a_log.astype(jnp.float32), d_skip.astype(jnp.float32), gate_gain.astype(jnp.float32), w_out.astype(jnp.float32))
    inputs_f = tokens.astype(jnp.float32)

    def whole(params, block_in):
        row_fn = jax.checkpoint(partial(branch_row, params))

        def one_row(row_pair):
            return row_fn(row_pair[0], row_pair[1])
        return lax.map(one_row, (block_in, lengths))
    block_out, back_fn = jax.vjp(whole, weights, inputs_f)
    grads, input_grad = back_fn(cotangent.astype(jnp.float32))
    return (block_out.astype(jnp.bfloat16), input_grad.astype(jnp.bfloat16), grads[0], grads[1], grads[2], grads[3], grads[4], grads[5], grads[6], grads[7], grads[8], grads[9], grads[10])
```

```python
import jax
import jax.numpy as jnp
from jax import lax
from jax.experimental import pallas as pl
from jax.experimental.pallas import tpu as pltpu
from jax.sharding import PartitionSpec as P

HEAD_DIM = 64
STATE = 128
CONV = 4
EPSILON = 1e-05
LOG2E = 1.4426950408889634
BLOCK = 256
SUB = 128
SUBS = BLOCK // SUB
LANES = 128
WIDE = 256
PIECE = 512
RIM = 16
F32 = jnp.float32
BF16 = jnp.bfloat16
VMEM_LIMIT = 65200 * 1024
MESH = pl.DeviceIdType.MESH
RATE, DT_BIAS, SKIP, REAL = range(4)


def dot(left, right):
    return jnp.dot(left, right, preferred_element_type=F32)


def dot_t(left, right):
    return lax.dot_general(left, right, (((1,), (1,)), ((), ())), preferred_element_type=F32)


def t_dot(left, right):
    return lax.dot_general(left, right, (((0,), (0,)), ((), ())), preferred_element_type=F32)


def split_dot(left, right):
    high = left.astype(BF16)
    low = (left - high.astype(F32)).astype(BF16)
    return dot(high, right) + dot(low, right)


def split_dot_t(left, right):
    high = left.astype(BF16)
    low = (left - high.astype(F32)).astype(BF16)
    return dot_t(high, right) + dot_t(low, right)


def flip(value):
    return value.astype(F32).T.astype(BF16)


def sigmoid(value):
    return 0.5 * jnp.tanh(0.5 * value) + 0.5


def fold(value):
    return jnp.sum(value.reshape(-1, 8, value.shape[1]), axis=0)


def grid2(size):
    return (
        lax.broadcasted_iota(jnp.int32, (size, size), 0),
        lax.broadcasted_iota(jnp.int32, (size, size), 1),
    )


def lower_ones(size):
    row, col = grid2(size)
    return jnp.where(row >= col, 1.0, 0.0).astype(BF16)


def half_mask():
    return lax.broadcasted_iota(jnp.int32, (SUB, LANES), 1) < HEAD_DIM


def pair_diag(value, first_half):
    zero = jnp.zeros_like(value)
    return jnp.concatenate(
        [jnp.where(first_half, value, zero), jnp.where(first_half, zero, value)], axis=0
    )


def set_spread(spread):
    row = lax.broadcasted_iota(jnp.int32, spread.shape, 0)
    head = lax.broadcasted_iota(jnp.int32, spread.shape, 1) // HEAD_DIM
    spread[...] = jnp.where((row % 32 == head) & (row < 96), 1.0, 0.0).astype(BF16)


def parts(value):
    value = jnp.where(lax.broadcasted_iota(jnp.int32, value.shape, 1) < 32, value, 0.0)
    high = value.astype(BF16).astype(F32)
    rest = value - high
    mid = rest.astype(BF16).astype(F32)
    low = (rest - mid).astype(BF16).astype(F32)
    return (high + pltpu.roll(mid, 32, 1) + pltpu.roll(low, 64, 1)).astype(BF16)


def tile(index, width=LANES):
    return pl.ds(pl.multiple_of(index * width, width), width)


def chunks(width):
    return [slice(start, start + WIDE) for start in range(0, width, WIDE)]


def norm_rows(rows):
    value = rows.astype(F32)
    return value, lax.rsqrt(jnp.mean(value * value, axis=-1, keepdims=True) + EPSILON)


def normed_of(rows, gain):
    value, rms = norm_rows(rows)
    return (value * rms * gain).astype(BF16)


def head_row(value):
    row = value.reshape(1, -1)
    return jnp.concatenate([row, jnp.zeros((1, LANES - row.shape[1]), F32)], axis=1)


def set_rate(heads, a_log_ref):
    heads[RATE : RATE + 1, :] = head_row(-jnp.exp(a_log_ref[...]) * LOG2E)


def set_conv(conv, weight_ref, bias_ref):
    conv[0:CONV, :] = weight_ref[...]
    conv[CONV : CONV + 1, :] = bias_ref[...].reshape(1, -1)


def set_step_weight(weight, wdt_ref):
    weight[...] = jnp.zeros_like(weight)
    weight[0 : wdt_ref.shape[0], :] = wdt_ref[...]


def places():
    dp, seq = lax.axis_index("dp"), lax.axis_index("seq")
    core_size = 2
    y_size = lax.axis_size("seq") // core_size
    x_size = y_size if lax.axis_size("dp") % y_size == 0 else 1
    z_size = lax.axis_size("dp") // x_size
    x, z = lax.rem(dp, x_size), lax.div(dp, x_size)
    core, y = lax.rem(seq, core_size), lax.div(seq, core_size)
    return {
        "core": (core_size, core, lambda p: {"dp": dp, "seq": y * core_size + p}),
        "y": (y_size, y, lambda p: {"dp": dp, "seq": p * core_size + core}),
        "x": (x_size, x, lambda p: {"dp": z * x_size + p, "seq": seq}),
        "z": (z_size, z, lambda p: {"dp": p * x_size + x, "seq": seq}),
        "seq": (lax.axis_size("seq"), seq, lambda p: {"dp": dp, "seq": p}),
    }


def axis_sizes():
    y_size = lax.axis_size("seq") // 2
    return [2, y_size, y_size, lax.axis_size("dp") // y_size]


def greet(axes, names):
    barrier = pltpu.get_barrier_semaphore()
    count = 0
    for name in names:
        size, index, at = axes[name]
        for k in range(1, size):
            pl.semaphore_signal(barrier, inc=1, device_id=at(lax.rem(index + k, size)), device_id_type=MESH)
            count += 1
    pl.semaphore_wait(barrier, count)


def state_copies(axes, value, slots, send_sems, recv_sems):
    size, index, at = axes["seq"]
    return [
        pltpu.make_async_remote_copy(
            src_ref=value,
            dst_ref=slots.at[index],
            send_sem=send_sems.at[k - 1],
            recv_sem=recv_sems.at[k - 1],
            device_id=at(lax.rem(index + k, size)),
            device_id_type=MESH,
        )
        for k in range(1, size)
    ]


def two_level(axes, value, pair, chip, chips, send_sems, recv_sems):
    _, core, at_core = axes["core"]
    size, y, at_y = axes["y"]
    width = value.shape[-1] // 2
    half = pl.ds(pl.multiple_of(core * width, LANES), width)

    def remote(source, target, device, n):
        return pltpu.make_async_remote_copy(
            src_ref=source, dst_ref=target, send_sem=send_sems.at[n], recv_sem=recv_sems.at[n],
            device_id=device, device_id_type=MESH,
        )

    first = [remote(value, pair, at_core(1 - core), 0)]
    second = [remote(chip, chips.at[y, :, half], at_y(lax.rem(y + k, size)), k) for k in range(1, size)]
    received = [chips.at[lax.rem(y + size - k, size), :, half] for k in range(1, size)]
    third = [remote(ref, ref, at_core(1 - core), size + n) for n, ref in enumerate(received)]
    return half, first, second, third


def shift_copy(axes, source, target, by, send_sem, recv_sem):
    size, index, at = axes["seq"]
    return pltpu.make_async_remote_copy(
        src_ref=source, dst_ref=target, send_sem=send_sem, recv_sem=recv_sem,
        device_id=at(lax.rem(index + by + size, size)), device_id_type=MESH,
    )


def padded(count, unit):
    return -(-count // unit) * unit


def piece_of(rows):
    return max(n for n in range(16, 513, 16) if rows % n == 0)


class Job:
    def __init__(self, src, dst, recv, recv_base, base, rows, order, axes, send_sems, recv_sems, own_sem):
        self.src, self.dst, self.recv = src, dst, recv
        self.send_sems, self.recv_sems = send_sems, recv_sems
        self.axes = [axes[name] for name in order]
        self.spans = [(base, rows)]
        self.slots = []
        for size, index, _ in self.axes:
            at, span = self.spans[-1]
            part = span // size
            self.spans.append((pl.multiple_of(at + index * part, 16), part))
            self.slots.append(recv_base)
            recv_base += (size - 1) * part
        self.stages = 2 * len(self.axes)
        self.end = base + rows
        own, part = self.spans[-1]
        self.result = recv.at[pl.ds(self.slots[-1], part)]
        self.keep = pltpu.make_async_copy(self.result, dst.at[pl.ds(own, part)], own_sem)

    def copies(self, stage):
        down = stage < len(self.axes)
        level = stage if down else self.stages - 1 - stage
        size, index, at = self.axes[level]
        base, _ = self.spans[level]
        own, part = self.spans[level + 1]
        result = []
        for k in range(1, size):
            partner = lax.rem(index + k, size)
            if down:
                if level == 0:
                    source = self.src.at[pl.ds(pl.multiple_of(base + partner * part, 16), part)]
                else:
                    held = self.slots[level - 1]
                    source = self.recv.at[pl.ds(pl.multiple_of(held + partner * part, 16), part)]
                target = self.recv.at[pl.ds(self.slots[level] + (k - 1) * part, part)]
            else:
                target = self.dst.at[pl.ds(own, part)]
                source = self.result if stage == len(self.axes) else target
            result.append(
                pltpu.make_async_remote_copy(
                    src_ref=source,
                    dst_ref=target,
                    send_sem=self.send_sems.at[stage, k - 1],
                    recv_sem=self.recv_sems.at[stage, k - 1],
                    device_id=at(partner),
                    device_id_type=MESH,
                )
            )
        return result

    def start(self, stage):
        for copy in self.copies(stage):
            copy.start()

    def move(self, stage):
        if stage > 0:
            self.finish(stage - 1)
        if stage < self.stages:
            self.start(stage)

    def finish(self, stage):
        for copy in self.copies(stage):
            copy.wait()
        if stage == len(self.axes):
            self.keep.wait()
        if stage >= len(self.axes):
            return
        size, index, _ = self.axes[stage]
        own, part = self.spans[stage + 1]
        slot = self.slots[stage]
        step = piece_of(part)

        @pl.loop(0, part // step)
        def _(i):
            def rows(start):
                return pl.ds(pl.multiple_of(start + i * step, 16), step)

            if stage == 0:
                total = self.src[rows(own), :].astype(F32)
            else:
                total = self.recv[rows(self.slots[stage - 1] + index * part), :].astype(F32)
            for k in range(size - 1):
                total = total + self.recv[rows(slot + k * part), :].astype(F32)
            self.recv[rows(slot), :] = total.astype(BF16)

        if stage == len(self.axes) - 1:
            self.keep.start()


class VectorJob:
    def __init__(self, total, recv, order, axes, send_sems, recv_sems):
        self.total, self.recv, self.send_sems, self.recv_sems = total, recv, send_sems, recv_sems
        self.axes = [axes[name] for name in order]
        self.slots = [sum(axis[0] for axis in self.axes[:i]) for i in range(len(self.axes))]

    def copies(self, stage):
        size, index, at = self.axes[stage]
        slot = self.slots[stage] + index
        return [
            pltpu.make_async_remote_copy(
                src_ref=self.recv.at[slot],
                dst_ref=self.recv.at[slot],
                send_sem=self.send_sems.at[stage, k - 1],
                recv_sem=self.recv_sems.at[stage, k - 1],
                device_id=at(lax.rem(index + k, size)),
                device_id_type=MESH,
            )
            for k in range(1, size)
        ]

    def start(self, stage):
        self.recv[self.slots[stage] + self.axes[stage][1]] = self.total[...]
        for copy in self.copies(stage):
            copy.start()

    def finish(self, stage):
        for copy in self.copies(stage):
            copy.wait()
        slot = self.slots[stage]
        total = self.recv[slot]
        for k in range(1, self.axes[stage][0]):
            total = total + self.recv[slot + k]
        self.total[...] = total


EARLY_JOBS = (9, 9, 9, 9)
LATE_JOBS = (3, 3, 3, 3, 3, 3, 2, 2)
MOST_JOBS = 8
ORDERS = (("core", "x", "y", "z"), ("core", "y", "x", "z"))
STAGES = 8


def jobs_of(sizes, src, dst, recv, axes, send_sems, recv_sems, own_sems):
    unit = 16 * lax.axis_size("dp") * lax.axis_size("seq")
    units = src.shape[0] // unit
    if sum(sizes) != units:
        sizes = [1] * units
    jobs = []
    base = 0
    for n, size in enumerate(sizes):
        rows = size * unit
        jobs.append(
            Job(
                src, dst, recv, base, base, rows, ORDERS[n % 2], axes, send_sems.at[n], recv_sems.at[n], own_sems.at[n]
            )
        )
        base += rows
    return jobs


def job_sems():
    return pltpu.SemaphoreType.DMA((JOBS, STAGES, max(axis_sizes()) - 1))


def pack_slabs(packed_ref, at, rows, first, value):
    count, width = value.shape
    for n in range(width // LANES):
        start = at + n * rows + first
        packed_ref[start : start + count, :] = value[:, n * LANES : (n + 1) * LANES].astype(BF16)


def enter_kernel(
    tok_ref, tail_ref, last_ref, gain_ref, wx_ref, wdt_in, weight_ref, bias_ref, dtb_ref, a_log_ref,
    normed_ref, xbc_ref, x_ref, bc_ref, dt_ref, sig_ref, added_ref, state_ref, logd_ref, xhalo_ref,
    product, spread, ext, state, suffix, prev, halo, xbc_send, xbc_halo, heads_ref, conv_ref, wdt_ref,
    halo_send, halo_recv, xbc_sems,
):
    step = pl.program_id(0)
    steps = pl.num_programs(0)
    inner = x_ref.shape[1]
    width = xbc_ref.shape[1]
    features = tok_ref.shape[2]
    axes = places()
    shift = shift_copy(axes, last_ref.at[0], halo, 1, halo_send, halo_recv)
    xbc_shift = shift_copy(axes, xbc_send, xbc_halo, 1, xbc_sems.at[0], xbc_sems.at[1])

    @pl.when(step == 0)
    def _():
        greet(axes, ("seq",))
        shift.start()
        set_spread(spread)
        set_rate(heads_ref, a_log_ref)
        heads_ref[DT_BIAS : DT_BIAS + 1, :] = head_row(dtb_ref[...])
        heads_ref[REAL : REAL + 1, :] = head_row(jnp.ones_like(dtb_ref))
        set_conv(conv_ref, weight_ref, bias_ref)
        set_step_weight(wdt_ref, wdt_in)
        state[...] = jnp.zeros_like(state)
        suffix[...] = jnp.zeros_like(suffix)

    @pl.when(step < steps - 1)
    def _():
        prev[...] = tail_ref[0]

    @pl.when(step == steps - 1)
    def _():
        shift.wait()
        prev[...] = jnp.where(axes["seq"][1] == 0, jnp.zeros_like(prev), halo[...])

    gain = gain_ref[...].reshape(1, -1)
    normed = normed_of(tok_ref[0], gain)
    both = jnp.concatenate([normed_of(prev[...], gain), normed], axis=0)
    normed_ref[...] = normed
    product[...] = dot(both, wx_ref[...])
    for n in range(width // LANES):
        lanes = slice(n * LANES, (n + 1) * LANES)
        part = product[:, lanes].astype(BF16)
        xbc_ref[:, lanes] = part[RIM:]
        ext[n] = part.astype(F32)

    @pl.when(step == 0)
    def _():
        xbc_send[...] = xbc_ref[BLOCK - RIM :, :]
        xbc_shift.start()

    real = heads_ref[REAL : REAL + 1, :]
    dt_raw = dot_t(normed, wdt_ref[...]) + heads_ref[DT_BIAS : DT_BIAS + 1, :]
    softplus = jnp.maximum(dt_raw, 0.0) + jnp.log1p(jnp.exp(-jnp.abs(dt_raw)))
    dt_low = (softplus * real).astype(BF16)
    dt_ref[...] = dt_low
    sig_ref[...] = sigmoid(dt_raw)

    def conv(lane, dst_ref, dst_lane):
        lanes = tile(lane)
        taps = [conv_ref[k : k + 1, lanes] for k in range(CONV)]
        bias = conv_ref[CONV : CONV + 1, lanes]
        for row in range(0, BLOCK, 64):
            total = bias
            for k in range(CONV):
                at = row + RIM - (CONV - 1) + k
                total = total + taps[k] * ext[lane, at : at + 64, :]
            dst_ref[row : row + 64, tile(dst_lane)] = (total * sigmoid(total)).astype(BF16)

    for lane in range(2):
        conv(inner // LANES + lane, bc_ref, lane)

    @pl.loop(0, inner // LANES)
    def _(lane):
        conv(lane, x_ref, lane)

    ones = lower_ones(SUB)
    factors = []
    finals = []
    for sub in range(SUBS):
        dt_sub = dt_low[sub * SUB : (sub + 1) * SUB]
        run = dot(ones, dt_sub) * heads_ref[RATE : RATE + 1, :]
        final = run[SUB - 1 : SUB]
        factors.append(parts(jnp.exp2(final - run) * dt_sub.astype(F32)))
        finals.append(parts(jnp.broadcast_to(final, (8, LANES))))
    b_flip = [flip(bc_ref[sub * SUB : (sub + 1) * SUB, :STATE]) for sub in range(SUBS)]
    product[:, :inner] = dot(jnp.concatenate(factors + finals, axis=0), spread[...])
    for sub in reversed(range(SUBS)):
        rows = slice(sub * SUB, (sub + 1) * SUB)
        at = SUBS * SUB + 8 * sub
        weighted = (product[rows, :inner] * x_ref[rows, :].astype(F32)).astype(BF16)
        added = dot(b_flip[sub], weighted)
        added_ref[sub] = added.astype(BF16)
        state[...] += jnp.exp2(suffix[0:1, :]) * added
        suffix[...] += product[at : at + 8, :inner]

    @pl.when(step == steps - 1)
    def _():
        state_ref[...] = state[...].astype(BF16)
        logd_ref[...] = suffix[...]
        xbc_shift.wait()
        xhalo_ref[...] = jnp.where(axes["seq"][1] == 0, jnp.zeros_like(xbc_halo), xbc_halo[...])


def middle_kernel(
    len_ref, tok_ref, cot_ref, normed_ref, x_ref, bc_ref, dt_ref, added_ref, state_ref, logd_ref,
    wz_ref, wo_ref, gain_ref, a_log_ref, skip_in,
    out_ref, gy_ref, gz_ref, starts_ref, rowdot_ref, adj_ref, pack_ref, ggain_ref, logds_ref, norm_t_ref,
    wide, spread, scan, state, prefix, skip, gate, go, o_all, gz_all, gb_all, norm_t, adj, ggain, pair_state, chip_state, chips, logds,
    heads_ref, gains_ref, slot_send, slot_recv, log_send, log_recv,
):
    step = pl.program_id(0)
    steps = pl.num_programs(0) // 2
    inner = x_ref.shape[1]
    features = tok_ref.shape[2]
    tok_rows = steps * BLOCK
    axes = places()
    count, me, _ = axes["seq"]
    core = axes["core"][1]
    y_count, y, _ = axes["y"]
    half, pair_copies, chip_copies, half_copies = two_level(
        axes, state_ref, pair_state, chip_state, chips, slot_send, slot_recv
    )
    pair_copies += state_copies(axes, logd_ref, logds, log_send, log_recv)
    ones = lower_ones(SUB)

    @pl.when(step == 0)
    def _():
        greet(axes, ("seq",))
        for copy in pair_copies:
            copy.start()
        logds[me] = logd_ref[...]
        set_spread(spread)
        set_rate(heads_ref, a_log_ref)
        heads_ref[SKIP : SKIP + 1, :] = head_row(skip_in[...])
        gains_ref[1:2, :] = gain_ref[...].reshape(1, -1)
        prefix[...] = jnp.zeros_like(prefix)
        adj[...] = jnp.zeros_like(adj)
        ggain[...] = jnp.zeros_like(ggain)
        for lanes in chunks(inner):
            skip[:, lanes] = dot(
                parts(jnp.broadcast_to(heads_ref[SKIP : SKIP + 1, :], (8, LANES))), spread[:, lanes]
            )

    @pl.when(step < steps)
    def _():
        row_i, col_i = grid2(SUB)
        causal = row_i >= col_i
        first_half = half_mask()
        for sub in range(SUBS):
            rows = slice(sub * SUB, (sub + 1) * SUB)
            dt_low = dt_ref[rows]
            meet = jnp.where(causal, dot_t(bc_ref[rows, STATE:], bc_ref[rows, :STATE]), 0.0)
            run = dot(ones, dt_low) * heads_ref[RATE : RATE + 1, :]
            run_t = run.T
            first_row = step * BLOCK + sub * SUB
            all_rows = pl.ds(pl.multiple_of(first_row, SUB), SUB)
            live = me * tok_rows + first_row + lax.broadcasted_iota(jnp.int32, (SUB, 1), 0) < len_ref[0]
            g_branch = jnp.where(live, cot_ref[0, rows, :], jnp.zeros((SUB, features), BF16))
            gb_all[all_rows, :] = g_branch
            normed = normed_ref[rows, :]
            norm_t[:, all_rows] = flip(normed)
            wide[:SUB, :] = dot(dt_low, spread[...])
            if sub == SUBS - 1:
                block_rows = tile(step, BLOCK)
                gate[block_rows, :] = dot(normed_ref[...], wz_ref[...])
                go[block_rows, :] = dot_t(gb_all[block_rows, :], wo_ref[...])
            for pair in range(inner // LANES):
                lanes = slice(pair * LANES, (pair + 1) * LANES)
                inflow = wide[:SUB, lanes] * x_ref[rows, lanes].astype(F32)
                scores = []
                for head in (2 * pair, 2 * pair + 1):
                    gap = jnp.minimum(run[:, head : head + 1] - run_t[head : head + 1, :], 0.0)
                    scores.append((jnp.exp2(gap) * meet).astype(BF16))
                scan[step, rows, lanes] = dot(
                    jnp.concatenate(scores, axis=1), pair_diag(inflow.astype(BF16), first_half)
                )

    @pl.when(step == 0)
    def _():
        for copy in pair_copies:
            copy.wait()
        mine, other = state_ref[:, half].astype(F32), pair_state[:, half].astype(F32)
        decay = jnp.exp2(logds[2 * y + 1, 0:1, half])
        chip_state[...] = jnp.where(core == 0, decay * mine + other, decay * other + mine).astype(BF16)
        for copy in chip_copies:
            copy.start()

    @pl.when(step == steps // 2)
    def _():
        for copy in chip_copies:
            copy.wait()
        for copy in half_copies:
            copy.start()

    @pl.when(step == steps)
    def _():
        for copy in half_copies:
            copy.wait()
        logds_ref[...] = logds[...]
        for lanes in chunks(inner):
            total = jnp.zeros((STATE, WIDE), F32)
            for chip in range(y_count):
                decay = jnp.exp2(logds[2 * chip, 0:1, lanes] + logds[2 * chip + 1, 0:1, lanes])
                total = jnp.where(chip < y, decay * total + chips[chip, :, lanes].astype(F32), total)
            decay = jnp.exp2(logds[2 * y, 0:1, lanes])
            state[:, lanes] = jnp.where(core == 1, decay * total + pair_state[:, lanes].astype(F32), total)

    @pl.when(step >= steps)
    def _():
        block = step - steps
        live = (
            me * tok_rows + block * BLOCK + lax.broadcasted_iota(jnp.int32, (BLOCK, 1), 0) < len_ref[0]
        )
        adj_factors = []
        for sub in range(SUBS):
            rows = slice(sub * SUB, (sub + 1) * SUB)
            c_out = bc_ref[rows, STATE:]
            run = dot(ones, dt_ref[rows]) * heads_ref[RATE : RATE + 1, :]
            final = run[SUB - 1 : SUB]
            factors = [parts(jnp.exp2(run)), parts(jnp.broadcast_to(jnp.exp2(final), (16, LANES)))]
            adj_factors.append(parts(jnp.exp2(run + prefix[0:1, :])))
            prefix[...] += final
            low = state[...].astype(BF16)
            starts_ref[sub] = low
            wide[...] = dot(jnp.concatenate(factors, axis=0), spread[...])
            scan[block, rows, :] += wide[:SUB, :] * dot(c_out, low)
            state[...] = wide[SUB : SUB + 1, :] * state[...] + added_ref[sub].astype(F32)
        base = pl.multiple_of(block * BLOCK, BLOCK)

        @pl.loop(0, BLOCK // 32)
        def _(chunk):
            rows = tile(chunk, 32)
            all_rows = pl.ds(pl.multiple_of(base + chunk * 32, 32), 32)
            square = jnp.zeros((32, LANES), F32)
            cross = jnp.zeros((32, LANES), F32)
            for lane in range(inner // LANES):
                lanes = slice(lane * LANES, (lane + 1) * LANES)
                y = (scan[block, rows, lanes] + skip[0:1, lanes] * x_ref[rows, lanes].astype(F32)).astype(BF16)
                o_all[all_rows, lanes] = y
                pre = gate[all_rows, lanes]
                gated = y.astype(F32) * (pre * sigmoid(pre))
                square += gated * gated
                cross += go[all_rows, lanes] * gains_ref[1:2, lanes] * gated
            rms = lax.rsqrt(jnp.sum(square, axis=-1, keepdims=True) * (1.0 / inner) + EPSILON)
            pull = jnp.sum(cross, axis=-1, keepdims=True) * (1.0 / inner) * rms * rms * rms
            rms = jnp.broadcast_to(rms, (32, LANES))
            pull = jnp.broadcast_to(pull, (32, LANES))
            for lane in range(inner // LANES):
                lanes = slice(lane * LANES, (lane + 1) * LANES)
                y = o_all[all_rows, lanes].astype(F32)
                pre = gate[all_rows, lanes]
                sig = sigmoid(pre)
                silu = pre * sig
                gated = y * silu
                gain = gains_ref[1:2, lanes]
                g_o = go[all_rows, lanes]
                unit = gated * rms
                o_all[all_rows, lanes] = (unit * gain).astype(BF16)
                ggain[:, lanes] += fold(g_o * unit)
                g_gated = rms * (g_o * gain) - pull * gated
                g_y = (g_gated * silu).astype(BF16)
                gy_ref[rows, lanes] = g_y
                g_z = (g_gated * y * (sig + silu * (1.0 - sig))).astype(BF16)
                gz_ref[rows, lanes] = g_z
                gz_all[all_rows, lanes] = g_z
                go[all_rows, lanes] = g_y.astype(F32) * scan[block, rows, lanes]

        branch = dot(o_all[tile(block, BLOCK), :], wo_ref[...])
        out_ref[0] = (tok_ref[0].astype(F32) + jnp.where(live, branch, 0.0)).astype(BF16)
        product = go[tile(block, BLOCK), :]
        high = product.astype(BF16)
        low = (product - high.astype(F32)).astype(BF16)
        head_sums = dot_t(jnp.concatenate([high, low], axis=0), spread[...])
        rowdot_ref[...] = head_sums[:BLOCK] + head_sums[BLOCK:]
        c_flip = jnp.concatenate([flip(bc_ref[sub * SUB : (sub + 1) * SUB, STATE:]) for sub in range(SUBS)], axis=1)
        factor = jnp.concatenate(adj_factors, axis=0)
        scaled = (dot(factor, spread[...]) * gy_ref[...].astype(F32)).astype(BF16)
        adj[...] += dot(c_flip, scaled)

    @pl.when(step == 2 * steps - 1)
    def _():
        norm_t_ref[...] = norm_t[...]
        adj_ref[...] = adj[...].astype(BF16)
        ggain_ref[...] = ggain[...]
        for lanes in chunks(inner):
            o_flip = flip(o_all[:, lanes])
            pack_slabs(pack_ref, 0, inner, lanes.start, dot(o_flip, gb_all[...]))
        for start in range(0, features, BLOCK):
            part = dot(norm_t[start : start + BLOCK, :], gz_all[...])
            pack_slabs(pack_ref, inner * features // LANES, features, start, part)
        used = 2 * inner * features // LANES
        if pack_ref.shape[0] > used:
            pack_ref[used:, :] = jnp.zeros((pack_ref.shape[0] - used, LANES), BF16)


def vector_rows(features, width, inner):
    counts = (features // LANES, CONV * width // LANES, width // LANES, inner // LANES, 1, 1, 1)
    starts = [sum(counts[:n]) for n in range(len(counts))]
    return starts, padded(sum(counts), 8)


def back_kernel(
    x_row, x_col, gy_row, gy_col, bc_ref, dt_ref, sig_ref, rowdot_ref, starts_ref, xbc_ref, xhalo_ref, xbc_rest, xhalo_rest, adj_ref,
    logds_ref, early_ref, ggain_ref, tok_ref, cot_ref, norm_t_in, gz_in, wz_in, wx_in, wdt_in,
    gain_ref, weight_ref, bias_ref, a_log_ref, skip_in,
    grad_ref, early_out, late_out, vec_out,
    spread, gather, ginf, factors, finals, c_flip, g_bc, x_ginf, column, d_final, skip, act, ext, gconv, gx_all, gdt_all,
    last, rim_send, rim_recv, gcw, gcb, gdtb, grate, gskip, gng, pair_adj, chip_adj, chips, early_recv, late_src, late_recv, vec, vec_recv,
    heads_ref, conv_ref, wdt_ref, norm_t, gz_ref, wz_ref, wx_ref,
    early_sems, late_sems, own_sems, vec_sems, slot_send, slot_recv, rim_sems, load_sems,
):
    step = pl.program_id(0)
    tok_rows, features = gx_all.shape[0], tok_ref.shape[2]
    inner = wz_ref.shape[1]
    width = wx_ref.shape[1]
    blocks = tok_rows // BLOCK
    subs = tok_rows // SUB
    pieces = inner // PIECE
    slab_rows = PIECE // LANES * features
    gn = ginf.at[:, pl.ds(0, features)]
    channel_step = blocks
    product_step = blocks + pieces
    norm_step = product_step + 1
    axes = places()
    count, me, _ = axes["seq"]
    core = axes["core"][1]
    y_count, y, _ = axes["y"]
    half, pair_copies, chip_copies, half_copies = two_level(
        axes, adj_ref, pair_adj, chip_adj, chips, slot_send, slot_recv
    )
    early = jobs_of(
        EARLY_JOBS, early_ref, early_out, early_recv, axes, early_sems.at[0], early_sems.at[1], own_sems.at[0]
    )
    late = jobs_of(LATE_JOBS, late_src, late_out, late_recv, axes, late_sems.at[0], late_sems.at[1], own_sems.at[1])
    vector = VectorJob(vec, vec_recv, ORDERS[0], axes, vec_sems.at[0], vec_sems.at[1])
    ones = lower_ones(SUB)
    row_i, col_i = grid2(SUB)
    later = row_i <= col_i

    loads = [
        pltpu.make_async_copy(source, target, load_sems.at[n])
        for n, (source, target) in enumerate(
            ((norm_t_in, norm_t), (gz_in, gz_ref), (wz_in, wz_ref), (wx_in, wx_ref))
        )
    ]

    channel_time = blocks * WITHIN_TIME
    product_time = channel_time + pieces * CHANNEL_TIME
    norm_time = product_time + PRODUCT_TIME
    end_time = norm_time + blocks * NORM_TIME
    moves = [
        (EARLY_PLAN[stage] + EARLY_SHIFT * (n // 2), job, stage)
        for n, job in enumerate(early)
        for stage in range(1, STAGES + 1)
    ]
    begins = []
    for job in late:
        piece = min((job.end - 1) // slab_rows, pieces)
        begins.append(piece + 1 + channel_step if piece < pieces else product_step)
        ready = channel_time + (piece + 1.3) * CHANNEL_TIME if piece < pieces else product_time + PRODUCT_TIME * 0.35
        moves += [(ready + LATE_PLAN[stage], job, stage) for stage in range(1, STAGES + 1)]
    moves.sort(key=lambda move: move[0])
    placed = []

    def advance(grid_step, since, until):
        due = [move for move in moves if since < move[0] <= until]
        placed.extend(due)
        if due:

            @pl.when(step == grid_step)
            def _():
                for _, job, stage in due:
                    job.move(stage)

    def advance_each(first, number, start, length, since, until):
        for n in range(number):
            base = start + n * length
            advance(first + n, base + since * length, base + until * length)

    @pl.when(step == 0)
    def _():
        greet(axes, ("seq", "x", "z"))
        for copy in pair_copies:
            copy.start()
        for job in early:
            job.start(0)
        for load in loads:
            load.start()
        set_spread(spread)
        for piece in range(inner // LANES):
            lanes = slice(piece * LANES, (piece + 1) * LANES)
            gather[lanes, :] = flip(spread[:, lanes])
        set_rate(heads_ref, a_log_ref)
        heads_ref[SKIP : SKIP + 1, :] = head_row(skip_in[...])
        set_conv(conv_ref, weight_ref, bias_ref)
        set_step_weight(wdt_ref, wdt_in)
        for lanes in chunks(inner):
            skip[:, lanes] = dot(
                parts(jnp.broadcast_to(heads_ref[SKIP : SKIP + 1, :], (8, LANES))), spread[:, lanes]
            )
        gconv[:, tok_rows:, :] = jnp.zeros((WIDE // LANES, 8, LANES), F32)
        for ref in (x_ginf, column, d_final, gcw, gcb, gdtb, grate, gskip, gng):
            ref[...] = jnp.zeros_like(ref)

    @pl.when(step < blocks)
    def _():
        first_half = half_mask()
        for sub in range(SUBS):
            rows = slice(sub * SUB, (sub + 1) * SUB)
            all_rows = pl.ds(pl.multiple_of(step * BLOCK + sub * SUB, SUB), SUB)
            number = step * SUBS + sub
            b_in, c_out = bc_ref[all_rows, :STATE], bc_ref[all_rows, STATE:]
            dt_low = dt_ref[all_rows, :]
            meet = jnp.where(later, dot_t(b_in, c_out), 0.0)
            run = dot(ones, dt_low) * heads_ref[RATE : RATE + 1, :]
            final = run[SUB - 1 : SUB]
            run_t = run.T
            factors[number] = jnp.concatenate(
                [dt_low, parts(jnp.exp2(final - run)), parts(jnp.exp2(run))], axis=0
            )
            finals[number] = parts(jnp.broadcast_to(jnp.exp2(final), (16, LANES)))
            c_flip[number] = flip(c_out)
            spread_dt = dot(dt_low, spread[...])
            g_meet = jnp.zeros((SUB, SUB), F32)
            for pair in range(inner // LANES):
                lanes = slice(pair * LANES, (pair + 1) * LANES)
                inflow = spread_dt[:, lanes] * x_row[rows, lanes].astype(F32)
                g_diag = pair_diag(gy_row[rows, lanes], first_half)
                g_scores = dot_t(inflow.astype(BF16), g_diag)
                scores = []
                for half, head in enumerate((2 * pair, 2 * pair + 1)):
                    decay = jnp.exp2(jnp.minimum(run_t[head : head + 1, :] - run[:, head : head + 1], 0.0))
                    scores.append((decay * meet).astype(BF16))
                    g_meet += decay * g_scores[:, half * SUB : (half + 1) * SUB]
                ginf[all_rows, lanes] = dot(jnp.concatenate(scores, axis=1), g_diag)
                if pair == inner // LANES // 2 - 1:
                    advance_each(0, blocks, 0.0, WITHIN_TIME, sub / SUBS, (sub + 0.5) / SUBS)
            g_meet = jnp.where(later, g_meet, 0.0).astype(BF16)
            g_bc[all_rows, :STATE] = dot(g_meet, c_out)
            g_bc[all_rows, STATE:] = t_dot(g_meet, b_in)
            advance_each(0, blocks, 0.0, WITHIN_TIME, (sub + 0.5) / SUBS, (sub + 1) / SUBS)

    @pl.when(step == 0)
    def _():
        for copy in pair_copies:
            copy.wait()
        mine, other = adj_ref[:, half].astype(F32), pair_adj[:, half].astype(F32)
        decay = jnp.exp2(logds_ref[2 * y, 0:1, half])
        chip_adj[...] = jnp.where(core == 0, mine + decay * other, other + decay * mine).astype(BF16)
        for copy in chip_copies:
            copy.start()

    @pl.when(step == blocks // 2)
    def _():
        for copy in chip_copies:
            copy.wait()
        for copy in half_copies:
            copy.start()

    @pl.when(step == channel_step)
    def _():
        for copy in half_copies:
            copy.wait()
        for load in loads:
            load.wait()

    def rim_copy(slot):
        return shift_copy(axes, rim_send.at[slot], rim_recv.at[slot], -1, rim_sems.at[0, slot], rim_sems.at[1, slot])

    def conv_back(slot, source, xbc, halo, at):
        for n in range(WIDE // LANES):
            lanes = slice(at + n * LANES, at + (n + 1) * LANES)
            ext[n, 0:RIM, :] = halo[:, lanes].astype(F32)
            ext[n, RIM:, :] = xbc[:, lanes].astype(F32)

        @pl.loop(0, WIDE // LANES)
        def _(n):
            lanes = tile(slot * (WIDE // LANES) + n)
            from_lanes = tile(at // LANES + n)
            taps = [conv_ref[k : k + 1, lanes] for k in range(CONV)]
            bias = conv_ref[CONV : CONV + 1, lanes]
            sums = [jnp.zeros((8, LANES), F32) for _ in range(CONV + 1)]
            for row in range(0, tok_rows, 64):
                start = row + RIM - (CONV - 1)
                shifted = [ext[n, start + k : start + k + 64, :] for k in range(CONV)]
                total = bias
                for k in range(CONV):
                    total = total + taps[k] * shifted[k]
                sig = sigmoid(total)
                g_act = source[row : row + 64, from_lanes].astype(F32)
                g_conv = g_act * (sig * (1.0 + total * (1.0 - sig)))
                gconv[n, row : row + 64, :] = g_conv
                for k in range(CONV):
                    sums[k] += fold(g_conv * shifted[k])
                sums[CONV] += fold(g_conv)
            for k in range(CONV):
                gcw[k, :, lanes] += sums[k]
            gcb[:, lanes] += sums[CONV]
            for row in range(0, tok_rows, 64):
                total = taps[CONV - 1] * gconv[n, row : row + 64, :]
                for k in range(CONV - 1):
                    start = row + CONV - 1 - k
                    total = total + taps[k] * gconv[n, start : start + 64, :]
                gx_all[row : row + 64, lanes] = total.astype(BF16)
            last[slot, :, tile(n)] = total[64 - RIM :]

        rim_send[slot] = gconv[:, 0:8, :]
        rim_copy(slot).start()

    def finish_slot(slot):
        rim_copy(slot).wait()
        row = lax.broadcasted_iota(jnp.int32, (8, LANES), 0)
        for n in range(WIDE // LANES):
            at = tile(slot * (WIDE // LANES) + n)
            rim = jnp.where(me == count - 1, jnp.zeros((8, LANES), F32), rim_recv[slot, n])
            fix = jnp.zeros((8, LANES), F32)
            for k in range(CONV - 1):
                moved = pltpu.roll(rim, 8 - CONV + 1 + k, 0)
                fix += jnp.where(row >= 8 - CONV + 1 + k, conv_ref[k : k + 1, at] * moved, 0.0)
            old = last[slot, :, n * LANES : (n + 1) * LANES]
            gx_all[tok_rows - RIM :, at] = jnp.concatenate([old[0:8], old[8:] + fix], axis=0).astype(BF16)

    def weight_gradient(piece, size):
        for m in range(features // BLOCK):
            part = dot(norm_t[m * BLOCK : (m + 1) * BLOCK, :], gx_all[:, pl.ds(pl.multiple_of(piece * PIECE, PIECE), size)])
            for n in range(size // LANES):
                at = pl.multiple_of(piece * slab_rows + n * features + m * BLOCK, 16)
                late_src[pl.ds(at, BLOCK), :] = part[:, n * LANES : (n + 1) * LANES].astype(BF16)

    def begin_late(last_piece):
        for job, begin in zip(late, begins):
            if ((job.end - 1) // slab_rows == pieces - 1) == last_piece and (job.end - 1) // slab_rows < pieces:

                @pl.when(step == begin)
                def _():
                    job.start(0)

    def finish_piece(piece, last_piece):
        for n in range(PIECE // WIDE):
            finish_slot(piece * (PIECE // WIDE) + n)
        weight_gradient(piece, PIECE)
        begin_late(last_piece)

    @pl.when((step >= channel_step) & (step < product_step))
    def _():
        piece = step - channel_step
        lanes = tile(piece, PIECE)
        spread_p = spread[:, lanes]
        gather_p = gather[lanes, :]
        skip_p = skip[0:1, lanes]
        after = jnp.zeros((STATE, PIECE), F32)
        for chip in reversed(range(y_count)):
            decay = jnp.exp2(logds_ref[2 * chip, 0:1, lanes] + logds_ref[2 * chip + 1, 0:1, lanes])
            after = jnp.where(chip > y, decay * after + chips[chip, :, lanes].astype(F32), after)
        decay = jnp.exp2(logds_ref[2 * y + 1, 0:1, lanes])
        after = jnp.where(core == 0, decay * after + pair_adj[:, lanes].astype(F32), after)
        skipped = [jnp.zeros((8, LANES), F32) for _ in range(PIECE // LANES)]
        for sub in reversed(range(subs)):
            rows = slice(sub * SUB, (sub + 1) * SUB)
            wide = dot(jnp.concatenate([factors[sub], finals[sub]], axis=0), spread_p)
            dt_e, to_end, from_start = wide[:SUB], wide[SUB : 2 * SUB], wide[2 * SUB : 3 * SUB]
            kept = wide[3 * SUB : 3 * SUB + 1]
            after_low = after.astype(BF16)
            start_low = starts_ref[sub]
            from_b = dot(bc_ref[rows, :STATE], after_low)
            operands = [[], [], [], [], []]
            block_sums = []
            for n in range(PIECE // LANES):
                at = slice(n * LANES, (n + 1) * LANES)
                columns = [[], [], [], [], []]
                block_sum = jnp.zeros((8, LANES), F32)
                skip_sum = jnp.zeros((8, LANES), F32)
                for row in range(0, SUB, 32):
                    here = slice(row, row + 32)
                    there = slice(sub * SUB + row, sub * SUB + row + 32)
                    x = x_col[there, at].astype(F32)
                    g_y = gy_col[there, at].astype(F32)
                    inflow = dt_e[here, at] * x
                    inflow_low = inflow.astype(BF16).astype(F32)
                    from_after = to_end[here, at] * from_b[here, at]
                    g_inflow = ginf[there, tile(piece * (PIECE // LANES) + n)] + from_after
                    act[there, at] = (dt_e[here, at] * g_inflow + skip_p[:, at] * g_y).astype(BF16)
                    product = inflow_low * g_inflow
                    high = product.astype(BF16)
                    columns[0].append((x * g_inflow).astype(BF16))
                    columns[1].append(high)
                    columns[2].append((product - high.astype(F32)).astype(BF16))
                    columns[3].append((from_start[here, at] * g_y).astype(BF16))
                    columns[4].append((to_end[here, at] * inflow).astype(BF16))
                    block_sum += fold(inflow_low * from_after)
                    skip_sum += fold(g_y * x)
                for operand, column_parts in zip(operands, columns):
                    operand.append(jnp.concatenate(column_parts, axis=0))
                block_sums.append(block_sum)
                skipped[n] += skip_sum
            x_g, high, low, scaled, weighted = [jnp.concatenate(operand, axis=1) for operand in operands]
            block_sum = jnp.concatenate(block_sums, axis=1) + kept * fold(
                start_low.astype(F32) * after_low.astype(F32)
            )
            sum_high = block_sum.astype(BF16).astype(F32)
            both = jnp.concatenate([sum_high, block_sum - sum_high], axis=0).astype(BF16)
            head_sums = dot(jnp.concatenate([x_g, high, low, both], axis=0), gather_p)
            x_ginf[rows, :] += head_sums[:SUB]
            column[rows, :] += head_sums[SUB : 2 * SUB] + head_sums[2 * SUB : 3 * SUB]
            d_final[sub] += head_sums[3 * SUB : 3 * SUB + 8] + head_sums[3 * SUB + 8 :]
            g_bc[rows, :STATE] += dot_t(weighted, after_low)
            g_bc[rows, STATE:] += dot_t(scaled, start_low)
            after = kept * after + dot(c_flip[sub], scaled)
            if sub == subs - 3:

                @pl.when(step > channel_step)
                def _():
                    finish_piece(piece - 1, False)

            done = (subs - sub) / subs * 0.7
            advance_each(channel_step, pieces, channel_time, CHANNEL_TIME, done - 0.7 / subs, done)
        gskip[:, lanes] += jnp.concatenate(skipped, axis=1)
        for n in range(PIECE // WIDE):
            conv_back(piece * (PIECE // WIDE) + n, act, xbc_ref, xhalo_ref, n * WIDE)
            since = 0.7 + 0.3 * n / (PIECE // WIDE)
            advance_each(
                channel_step, pieces, channel_time, CHANNEL_TIME, since, since + 0.3 / (PIECE // WIDE) + 1e-6
            )

    @pl.when(step == product_step)
    def _():
        conv_back(inner // WIDE, g_bc, xbc_rest, xhalo_rest, 0)
        finish_piece(pieces - 1, True)
        upper = jnp.where(later, 1.0, 0.0).astype(BF16)
        rate = heads_ref[RATE : RATE + 1, :] * (1.0 / LOG2E)
        rest = jnp.concatenate(
            [rowdot_ref[sub * SUB : (sub + 1) * SUB, :] - column[sub * SUB : (sub + 1) * SUB, :] for sub in range(subs)],
            axis=1,
        )
        sums = jnp.zeros_like(rest)
        for _ in range(3):
            part = rest.astype(BF16)
            sums += dot(upper, part)
            rest = rest - part.astype(F32)
        for sub in range(subs):
            rows = slice(sub * SUB, (sub + 1) * SUB)
            dt_f = dt_ref[rows, :].astype(F32)
            d_log = sums[:, sub * LANES : (sub + 1) * LANES]
            d_log = d_log + jnp.sum(d_final[sub], axis=0, keepdims=True)
            g_dt = (x_ginf[rows, :] + rate * d_log).astype(BF16).astype(F32)
            g_pre = g_dt * sig_ref[rows, :]
            gdt_all[rows, :] = g_pre.astype(BF16)
            gdtb[...] += fold(g_pre)
            grate[...] += fold(dt_f * d_log)
        advance(product_step, product_time, product_time + 0.2 * PRODUCT_TIME)
        finish_slot(inner // WIDE)
        weight_gradient(pieces, WIDE)
        at = width // LANES * features
        pack_slabs(late_src, at, 32, 0, dot_t(flip(gdt_all[...])[:32], norm_t[...]))
        used = at + 32 * features // LANES
        if late_src.shape[0] > used:
            late_src[used:, :] = jnp.zeros((late_src.shape[0] - used, LANES), BF16)
        for job in late:
            if (job.end - 1) // slab_rows >= pieces:
                job.start(0)
        for m in range(blocks):
            rows = slice(m * BLOCK, (m + 1) * BLOCK)
            gn[rows, :] = (
                dot_t(gz_ref[rows, :], wz_ref[...])
                + dot_t(gx_all[rows, :], wx_ref[...])
                + dot(gdt_all[rows, :], wdt_ref[...])
            )
            since = 0.2 if m == 0 else 0.4 + 0.6 * m / blocks
            until = 0.4 + 0.6 * (m + 1) / blocks
            advance(
                product_step, product_time + since * PRODUCT_TIME,
                product_time + until * PRODUCT_TIME if m < blocks - 1 else norm_time,
            )

    @pl.when(step >= norm_step)
    def _():
        block = step - norm_step
        rows = tile(block, BLOCK)
        g_normed = gn[rows, :]
        residual, rms = norm_rows(tok_ref[0])
        unit = residual * rms
        gng[...] += fold(g_normed * unit)
        h = g_normed * gain_ref[...].reshape(1, -1)
        pull = jnp.sum(h * unit, axis=-1, keepdims=True) * (1.0 / features)
        grad_ref[0] = (cot_ref[0].astype(F32) + rms * (h - unit * pull)).astype(BF16)
        advance_each(norm_step, blocks, norm_time, NORM_TIME, 0.0, 1.0)

    @pl.when(step == norm_step + blocks - 1)
    def _():
        starts, _ = vector_rows(features, width, inner)

        def put(row, ref):
            value = ref if ref.shape[0] == 1 else jnp.sum(ref, axis=0, keepdims=True)
            for n in range(value.shape[1] // LANES):
                vec[row + n : row + n + 1, :] = value[:, n * LANES : (n + 1) * LANES]

        vec[...] = jnp.zeros_like(vec)
        put(starts[0], gng[...])
        for k in range(CONV):
            put(starts[1] + k * width // LANES, gcw[k])
        put(starts[2], gcb[...])
        put(starts[3], ggain_ref[...])
        put(starts[4], gdtb[...])
        put(starts[5], grate[...] * (heads_ref[RATE : RATE + 1, :] * (1.0 / LOG2E)))
        put(starts[6], split_dot_t(gskip[...], spread[...]))
        vector.start(0)
        rest = [move for move in moves if move[0] > end_time]
        assert len(placed) + len(rest) == len(moves)
        for n, (_, job, stage) in enumerate(rest):
            job.move(stage)
            level, turn = divmod(n + 1, max(1, len(rest) // 5))
            if turn == 0 and level <= 4:
                vector.finish(level - 1)
                if level < 4:
                    vector.start(level)
        vec_out[...] = vec[...]


WITHIN_TIME = 5.0
CHANNEL_TIME = 12.0
PRODUCT_TIME = 14.0
NORM_TIME = 1.2
EARLY_PLAN = (0, 6, 17, 25, 36, 46, 54, 65, 71)
EARLY_SHIFT = 8
LATE_PLAN = (0, 4, 9, 13, 18, 23, 27, 32, 36)


def unpack_kernel(
    wo_ref, wz_ref, wx_ref, wdt_ref, vec_ref, out_in, grad_in,
    out_ref, grad_ref, gwo_ref, gwz_ref, gwx_ref, gwdt_ref, gng_ref, gcw_ref, gcb_ref, gdtb_ref, ga_ref, gskip_ref, ggain_ref,
):
    def slabs(source, target):
        rows = target.shape[0]
        for n in range(target.shape[1] // LANES):
            target[:, n * LANES : (n + 1) * LANES] = source[n * rows : (n + 1) * rows, :].astype(F32)

    out_ref[...] = out_in[...]
    grad_ref[...] = grad_in[...]
    slabs(wo_ref, gwo_ref)
    slabs(wz_ref, gwz_ref)
    slabs(wx_ref, gwx_ref)

    @pl.when(pl.program_id(0) == 0)
    def _():
        heads, features = gwdt_ref.shape
        width = gcb_ref.shape[0]
        at, _ = vector_rows(features, width, ggain_ref.shape[0])
        for n in range(features // LANES):
            gwdt_ref[:, n * LANES : (n + 1) * LANES] = wdt_ref[n * 32 : n * 32 + heads, :].astype(F32)

        def rows(start, size):
            return jnp.concatenate([vec_ref[start + n : start + n + 1, :] for n in range(size // LANES)], axis=1)

        gng_ref[...] = rows(at[0], features).reshape(-1)
        for k in range(CONV):
            gcw_ref[k : k + 1, :] = rows(at[1] + k * width // LANES, width)
        gcb_ref[...] = rows(at[2], width).reshape(-1)
        ggain_ref[...] = rows(at[3], ggain_ref.shape[0]).reshape(-1)
        for n, ref in enumerate((gdtb_ref, ga_ref, gskip_ref)):
            ref[...] = vec_ref[at[4 + n] : at[4 + n] + 1, :][0, :heads]


def unpack(early, late, vec, out, grad, inner, width, features, heads):
    sds = jax.ShapeDtypeStruct
    grid = width // WIDE
    last = inner // WIDE - 1
    first = inner * features // LANES // (2 * features)
    stop = width // LANES * features
    rest = 32 * features // LANES
    passed = pl.BlockSpec((1, BLOCK, features), lambda i: (0, jnp.minimum(i, out.shape[1] // BLOCK - 1), 0))
    vectors = [(heads, features), (features,), (CONV, width), (width,), (heads,), (heads,), (heads,), (inner,)]
    return pl.pallas_call(
        unpack_kernel,
        grid=(grid,),
        in_specs=[
            pl.BlockSpec((inner, LANES), lambda i: (jnp.minimum(i, features // LANES - 1), 0)),
            pl.BlockSpec((2 * features, LANES), lambda i: (first + jnp.minimum(i, last), 0)),
            pl.BlockSpec((2 * features, LANES), lambda i: (i, 0)),
            pl.BlockSpec((rest, LANES), lambda i: (stop // rest, 0)),
            whole(vec.shape), passed, passed,
        ],
        out_specs=[
            passed, passed,
            pl.BlockSpec((inner, LANES), lambda i: (0, jnp.minimum(i, features // LANES - 1))),
            pl.BlockSpec((features, WIDE), lambda i: (0, jnp.minimum(i, last))),
            pl.BlockSpec((features, WIDE), lambda i: (0, i)),
            *[whole(shape) for shape in vectors],
        ],
        out_shape=[
            sds(out.shape, BF16), sds(grad.shape, BF16),
            sds((inner, features), F32), sds((features, inner), F32), sds((features, width), F32),
            *[sds(shape, F32) for shape in vectors],
        ],
        compiler_params=pltpu.CompilerParams(vmem_limit_bytes=VMEM_LIMIT),
        name="unpack",
    )(early, early, late, late, vec, out, grad)


def whole(shape):
    return pl.BlockSpec(shape, lambda i: (0,) * len(shape), pipeline_mode=pl.Buffered(1))


def params(collective_id):
    return pltpu.CompilerParams(
        vmem_limit_bytes=VMEM_LIMIT, dimension_semantics=("arbitrary",), collective_id=collective_id, has_side_effects=True
    )


def local(
    tokens, lengths, cotangent, norm_gain, w_z, w_xbc, w_dt, conv_weight, conv_bias, dt_bias, a_log, d_skip, gate_gain, w_out
):
    tok_rows, features = tokens.shape[1:]
    inner = w_z.shape[1]
    width = w_xbc.shape[1]
    heads = a_log.shape[0]
    steps = tok_rows // BLOCK
    seq_count = lax.axis_size("seq")
    devices = lax.axis_size("dp") * seq_count
    sds = jax.ShapeDtypeStruct
    dma = pltpu.SemaphoreType.DMA

    head_scratch = [pltpu.VMEM((8, LANES), F32)]

    def rows3(n, at, single=False):
        return pl.BlockSpec((1, BLOCK, n), lambda i: (0, at(i), 0), pipeline_mode=pl.Buffered(1 if single else 2))

    def rows2(n, at, single=False):
        return pl.BlockSpec((BLOCK, n), lambda i: (at(i), 0), pipeline_mode=pl.Buffered(1 if single else 2))

    def tail_at(block):
        return jnp.maximum(block * (BLOCK // RIM) - 1, 0)

    def back(i):
        return steps - 1 - i

    normed, xbc, x, bc, dt, sig, added, state, logd, xbc_halo = pl.pallas_call(
        enter_kernel,
        grid=(steps,),
        in_specs=[
            rows3(features, back),
            pl.BlockSpec((1, RIM, features), lambda i: (0, tail_at(back(i)), 0)),
            pl.BlockSpec((1, RIM, features), lambda i: (0, tok_rows // RIM - 1, 0), pipeline_mode=pl.Buffered(1)),
            whole((features,)), whole((features, width)), whole((heads, features)), whole((CONV, width)), whole((width,)),
            whole((heads,)), whole((heads,)),
        ],
        out_specs=[
            rows2(features, back), rows2(width, back), rows2(inner, back), rows2(2 * STATE, back), rows2(LANES, back),
            rows2(LANES, back), pl.BlockSpec((SUBS, STATE, inner), lambda i: (back(i), 0, 0)),
            whole((STATE, inner)), whole((8, inner)), whole((RIM, width)),
        ],
        out_shape=[
            sds((tok_rows, features), BF16), sds((tok_rows, width), BF16), sds((tok_rows, inner), BF16),
            sds((tok_rows, 2 * STATE), BF16), sds((tok_rows, LANES), BF16), sds((tok_rows, LANES), F32),
            sds((tok_rows // SUB, STATE, inner), BF16), sds((STATE, inner), BF16), sds((8, inner), F32),
            sds((RIM, width), BF16),
        ],
        scratch_shapes=[
            pltpu.VMEM((BLOCK + RIM, width), F32),
            pltpu.VMEM((LANES, inner), BF16), pltpu.VMEM((width // LANES, BLOCK + RIM, LANES), F32),
            pltpu.VMEM((STATE, inner), F32), pltpu.VMEM((8, inner), F32), pltpu.VMEM((RIM, features), BF16),
            pltpu.VMEM((RIM, features), BF16), pltpu.VMEM((RIM, width), BF16), pltpu.VMEM((RIM, width), BF16), *head_scratch, pltpu.VMEM((8, width), F32),
            pltpu.VMEM((LANES, features), BF16), dma, dma, dma((2,)),
        ],
        compiler_params=params(0),
        name="enter",
    )(tokens, tokens, tokens, norm_gain, w_xbc, w_dt.T, conv_weight, conv_bias, dt_bias, a_log)

    count = seq_count - 1
    early_rows = padded(2 * inner * features // LANES, 16 * devices)
    late_rows = padded((width + 32) * features // LANES, 16 * devices)

    def either(i):
        return lax.rem(i, steps)

    def second(i):
        return jnp.maximum(i - steps, 0)

    out, g_y, g_z, starts, rowdot, adj, early, g_gain, logds, norm_t = pl.pallas_call(
        middle_kernel,
        grid=(2 * steps,),
        in_specs=[
            pl.BlockSpec(memory_space=pltpu.SMEM),
            rows3(features, second), rows3(features, either), rows2(features, either), rows2(inner, either),
            rows2(2 * STATE, either), rows2(LANES, either),
            pl.BlockSpec((SUBS, STATE, inner), lambda i: (second(i), 0, 0)), whole((STATE, inner)), whole((8, inner)),
            whole((features, inner)), whole((inner, features)), whole((inner,)), whole((heads,)), whole((heads,)),
        ],
        out_specs=[
            rows3(features, second), rows2(inner, second), rows2(inner, second),
            pl.BlockSpec((SUBS, STATE, inner), lambda i: (second(i), 0, 0)),
            rows2(LANES, second), whole((STATE, inner)), whole((early_rows, LANES)), whole((8, inner)),
            whole((seq_count, 8, inner)), whole((features, tok_rows)),
        ],
        out_shape=[
            sds((1, tok_rows, features), BF16), sds((tok_rows, inner), BF16), sds((tok_rows, inner), BF16),
            sds((tok_rows // SUB, STATE, inner), BF16), sds((tok_rows, LANES), F32),
            sds((STATE, inner), BF16), sds((early_rows, LANES), BF16), sds((8, inner), F32),
            sds((seq_count, 8, inner), F32), sds((features, tok_rows), BF16),
        ],
        scratch_shapes=[
            pltpu.VMEM((SUB + 16, inner), F32),
            pltpu.VMEM((LANES, inner), BF16), pltpu.VMEM((steps, BLOCK, inner), F32), pltpu.VMEM((STATE, inner), F32),
            pltpu.VMEM((8, LANES), F32), pltpu.VMEM((8, inner), F32), pltpu.VMEM((tok_rows, inner), F32),
            pltpu.VMEM((tok_rows, inner), F32), pltpu.VMEM((tok_rows, inner), BF16), pltpu.VMEM((tok_rows, inner), BF16),
            pltpu.VMEM((tok_rows, features), BF16), pltpu.VMEM((features, tok_rows), BF16),
            pltpu.VMEM((STATE, inner), F32), pltpu.VMEM((8, inner), F32),
            pltpu.VMEM((STATE, inner), BF16), pltpu.VMEM((STATE, inner // 2), BF16),
            pltpu.VMEM((seq_count // 2, STATE, inner), BF16), pltpu.VMEM((seq_count, 8, inner), F32),
            *head_scratch, pltpu.VMEM((8, inner), F32), dma((seq_count,)), dma((seq_count,)), dma((count,)), dma((count,)),
        ],
        compiler_params=params(1),
        name="middle",
    )(lengths, tokens, cotangent, normed, x, bc, dt, added, state, logd, w_z, w_out, gate_gain, a_log, d_skip)

    pieces = inner // PIECE
    norm_step = steps + pieces + 1

    def first(i):
        return jnp.minimum(i, steps - 1)

    def column(rows, most):
        return pl.BlockSpec((rows, PIECE), lambda i: (0, jnp.clip(i - steps, 0, most)))

    def rest(rows):
        return pl.BlockSpec((rows, WIDE), lambda i: (0, inner // WIDE), pipeline_mode=pl.Buffered(1))

    def final(i):
        return jnp.clip(i - norm_step, 0, steps - 1)

    _, vec_rows = vector_rows(features, width, inner)
    sizes = axis_sizes()
    reach = max(sizes) - 1
    tiles = WIDE // LANES
    grad, early, late, vec = pl.pallas_call(
        back_kernel,
        grid=(norm_step + steps,),
        in_specs=[
            rows2(inner, first, True), column(tok_rows, pieces - 1), rows2(inner, first, True), column(tok_rows, pieces - 1),
            whole((tok_rows, 2 * STATE)), whole((tok_rows, LANES)), whole((tok_rows, LANES)), whole((tok_rows, LANES)),
            pl.BlockSpec((tok_rows // SUB, STATE, PIECE), lambda i: (0, 0, jnp.clip(i - steps, 0, pieces - 1))),
            column(tok_rows, pieces - 1), column(RIM, pieces - 1), rest(tok_rows), rest(RIM),
            whole((STATE, inner)), whole((seq_count, 8, inner)), whole((early_rows, LANES)), whole((8, inner)),
            rows3(features, final, True), rows3(features, final, True), *[pl.BlockSpec(memory_space=pl.ANY)] * 4,
            whole((heads, features)), whole((features,)),
            whole((CONV, width)), whole((width,)), whole((heads,)), whole((heads,)),
        ],
        out_specs=[
            rows3(features, final), pl.BlockSpec(memory_space=pl.ANY), pl.BlockSpec(memory_space=pl.ANY),
            whole((vec_rows, LANES)),
        ],
        out_shape=[
            sds((1, tok_rows, features), BF16), sds((early_rows, LANES), BF16), sds((late_rows, LANES), BF16),
            sds((vec_rows, LANES), F32),
        ],
        scratch_shapes=[
            pltpu.VMEM((LANES, inner), BF16), pltpu.VMEM((inner, LANES), BF16), pltpu.VMEM((tok_rows, inner), F32),
            pltpu.VMEM((tok_rows // SUB, 3 * SUB, LANES), BF16), pltpu.VMEM((tok_rows // SUB, 16, LANES), BF16),
            pltpu.VMEM((tok_rows // SUB, STATE, SUB), BF16), pltpu.VMEM((tok_rows, 2 * STATE), F32),
            pltpu.VMEM((tok_rows, LANES), F32), pltpu.VMEM((tok_rows, LANES), F32),
            pltpu.VMEM((tok_rows // SUB, 8, LANES), F32), pltpu.VMEM((8, inner), F32),
            pltpu.VMEM((tok_rows, PIECE), BF16), pltpu.VMEM((tiles, tok_rows + RIM, LANES), F32),
            pltpu.VMEM((tiles, tok_rows + 8, LANES), F32), pltpu.VMEM((tok_rows, width), BF16),
            pltpu.VMEM((tok_rows, LANES), BF16), pltpu.VMEM((width // WIDE, RIM, WIDE), F32),
            pltpu.VMEM((width // WIDE, tiles, 8, LANES), F32), pltpu.VMEM((width // WIDE, tiles, 8, LANES), F32),
            pltpu.VMEM((CONV, 8, width), F32), pltpu.VMEM((8, width), F32), pltpu.VMEM((8, LANES), F32),
            pltpu.VMEM((8, LANES), F32), pltpu.VMEM((8, inner), F32), pltpu.VMEM((8, features), F32),
            pltpu.VMEM((STATE, inner), BF16), pltpu.VMEM((STATE, inner // 2), BF16),
            pltpu.VMEM((seq_count // 2, STATE, inner), BF16), pltpu.VMEM((early_rows, LANES), BF16),
            pltpu.VMEM((late_rows, LANES), BF16), pltpu.VMEM((late_rows, LANES), BF16),
            pltpu.VMEM((vec_rows, LANES), F32), pltpu.VMEM((sum(sizes), vec_rows, LANES), F32),
            *head_scratch, pltpu.VMEM((8, width), F32), pltpu.VMEM((LANES, features), BF16),
            pltpu.VMEM((features, tok_rows), BF16), pltpu.VMEM((tok_rows, inner), BF16),
            pltpu.VMEM((features, inner), BF16), pltpu.VMEM((features, width), BF16),
            dma((2, MOST_JOBS, STAGES, reach)), dma((2, MOST_JOBS, STAGES, reach)), dma((2, MOST_JOBS)),
            dma((2, 4, reach)), dma((seq_count,)), dma((seq_count,)), dma((2, width // WIDE)), dma((4,)),
        ],
        compiler_params=params(2),
        name="back",
    )(
        x, x, g_y, g_y, bc, dt, sig, rowdot, starts, xbc, xbc_halo, xbc, xbc_halo, adj, logds, early, g_gain,
        tokens, cotangent, norm_t, g_z, w_z, w_xbc, w_dt.T, norm_gain, conv_weight, conv_bias, a_log, d_skip,
    )

    out, grad, g_wo, g_wz, g_wx, g_wdt, g_ng, g_cw, g_cb, g_dtb, g_a, g_skip, g_gain = unpack(
        early, late, vec, out, grad, inner, width, features, heads
    )
    return out, grad, g_ng, g_wz, g_wx, g_wdt.T, g_cw, g_cb, g_dtb, g_a, g_skip, g_gain, g_wo


def solution(mesh):
    rows = P("dp", "seq", None)
    return jax.shard_map(
        local,
        mesh=mesh,
        in_specs=(rows, P("dp"), rows) + (P(),) * 11,
        out_specs=(rows, rows) + (P(),) * 11,
        check_vma=False,
    )
```

```python
import jax
import jax.numpy as jnp
from jax import lax
from jax.experimental import pallas as pl
from jax.experimental.pallas import tpu as pltpu
from jax.sharding import PartitionSpec as P

HEAD_DIM = 64
STATE = 128
CONV = 4
EPSILON = 1e-05
LOG2E = 1.4426950408889634
BLOCK = 256
SUB = 128
SUBS = BLOCK // SUB
LANES = 128
WIDE = 256
PIECE = 512
RIM = 16
F32 = jnp.float32
BF16 = jnp.bfloat16
VMEM_LIMIT = 65200 * 1024
MESH = pl.DeviceIdType.MESH
RATE, DT_BIAS, SKIP, REAL = range(4)


def dot(left, right):
    return jnp.dot(left, right, preferred_element_type=F32)


def dot_t(left, right):
    return lax.dot_general(left, right, (((1,), (1,)), ((), ())), preferred_element_type=F32)


def t_dot(left, right):
    return lax.dot_general(left, right, (((0,), (0,)), ((), ())), preferred_element_type=F32)


def split_dot(left, right):
    high = left.astype(BF16)
    low = (left - high.astype(F32)).astype(BF16)
    return dot(high, right) + dot(low, right)


def split_dot_t(left, right):
    high = left.astype(BF16)
    low = (left - high.astype(F32)).astype(BF16)
    return dot_t(high, right) + dot_t(low, right)


def flip(value):
    return value.astype(F32).T.astype(BF16)


def sigmoid(value):
    return 0.5 * jnp.tanh(0.5 * value) + 0.5


def fold(value):
    return jnp.sum(value.reshape(-1, 8, value.shape[1]), axis=0)


def grid2(size):
    return (
        lax.broadcasted_iota(jnp.int32, (size, size), 0),
        lax.broadcasted_iota(jnp.int32, (size, size), 1),
    )


def lower_ones(size):
    row, col = grid2(size)
    return jnp.where(row >= col, 1.0, 0.0).astype(BF16)


def half_mask():
    return lax.broadcasted_iota(jnp.int32, (SUB, LANES), 1) < HEAD_DIM


def pair_diag(value, first_half):
    zero = jnp.zeros_like(value)
    return jnp.concatenate(
        [jnp.where(first_half, value, zero), jnp.where(first_half, zero, value)], axis=0
    )


def set_spread(spread):
    row = lax.broadcasted_iota(jnp.int32, spread.shape, 0)
    head = lax.broadcasted_iota(jnp.int32, spread.shape, 1) // HEAD_DIM
    spread[...] = jnp.where((row % 32 == head) & (row < 96), 1.0, 0.0).astype(BF16)


def parts(value):
    value = jnp.where(lax.broadcasted_iota(jnp.int32, value.shape, 1) < 32, value, 0.0)
    high = value.astype(BF16).astype(F32)
    rest = value - high
    mid = rest.astype(BF16).astype(F32)
    low = (rest - mid).astype(BF16).astype(F32)
    return (high + pltpu.roll(mid, 32, 1) + pltpu.roll(low, 64, 1)).astype(BF16)


def tile(index, width=LANES):
    return pl.ds(pl.multiple_of(index * width, width), width)


def chunks(width):
    return [slice(start, start + WIDE) for start in range(0, width, WIDE)]


def norm_rows(rows):
    value = rows.astype(F32)
    return value, lax.rsqrt(jnp.mean(value * value, axis=-1, keepdims=True) + EPSILON)


def normed_of(rows, gain):
    value, rms = norm_rows(rows)
    return (value * rms * gain).astype(BF16)


def head_row(value):
    row = value.reshape(1, -1)
    return jnp.concatenate([row, jnp.zeros((1, LANES - row.shape[1]), F32)], axis=1)


def set_rate(heads, a_log_ref):
    heads[RATE : RATE + 1, :] = head_row(-jnp.exp(a_log_ref[...]) * LOG2E)


def set_conv(conv, weight_ref, bias_ref):
    conv[0:CONV, :] = weight_ref[...]
    conv[CONV : CONV + 1, :] = bias_ref[...].reshape(1, -1)


def set_step_weight(weight, wdt_ref):
    weight[...] = jnp.zeros_like(weight)
    weight[0 : wdt_ref.shape[0], :] = wdt_ref[...]


def places():
    dp, seq = lax.axis_index("dp"), lax.axis_index("seq")
    core_size = 2
    y_size = lax.axis_size("seq") // core_size
    x_size = y_size if lax.axis_size("dp") % y_size == 0 else 1
    z_size = lax.axis_size("dp") // x_size
    x, z = lax.rem(dp, x_size), lax.div(dp, x_size)
    core, y = lax.rem(seq, core_size), lax.div(seq, core_size)
    return {
        "core": (core_size, core, lambda p: {"dp": dp, "seq": y * core_size + p}),
        "y": (y_size, y, lambda p: {"dp": dp, "seq": p * core_size + core}),
        "x": (x_size, x, lambda p: {"dp": z * x_size + p, "seq": seq}),
        "z": (z_size, z, lambda p: {"dp": p * x_size + x, "seq": seq}),
        "seq": (lax.axis_size("seq"), seq, lambda p: {"dp": dp, "seq": p}),
    }


def axis_sizes():
    y_size = lax.axis_size("seq") // 2
    return [2, y_size, y_size, lax.axis_size("dp") // y_size]


def greet(axes, names):
    barrier = pltpu.get_barrier_semaphore()
    count = 0
    for name in names:
        size, index, at = axes[name]
        for k in range(1, size):
            pl.semaphore_signal(barrier, inc=1, device_id=at(lax.rem(index + k, size)), device_id_type=MESH)
            count += 1
    pl.semaphore_wait(barrier, count)


def state_copies(axes, value, slots, send_sems, recv_sems):
    size, index, at = axes["seq"]
    return [
        pltpu.make_async_remote_copy(
            src_ref=value,
            dst_ref=slots.at[index],
            send_sem=send_sems.at[k - 1],
            recv_sem=recv_sems.at[k - 1],
            device_id=at(lax.rem(index + k, size)),
            device_id_type=MESH,
        )
        for k in range(1, size)
    ]


def two_level(axes, value, pair, chip, chips, send_sems, recv_sems):
    _, core, at_core = axes["core"]
    size, y, at_y = axes["y"]
    width = value.shape[-1] // 2
    half = pl.ds(pl.multiple_of(core * width, LANES), width)

    def remote(source, target, device, n):
        return pltpu.make_async_remote_copy(
            src_ref=source, dst_ref=target, send_sem=send_sems.at[n], recv_sem=recv_sems.at[n],
            device_id=device, device_id_type=MESH,
        )

    first = [remote(value, pair, at_core(1 - core), 0)]
    second = [remote(chip, chips.at[y, :, half], at_y(lax.rem(y + k, size)), k) for k in range(1, size)]
    received = [chips.at[lax.rem(y + size - k, size), :, half] for k in range(1, size)]
    third = [remote(ref, ref, at_core(1 - core), size + n) for n, ref in enumerate(received)]
    return half, first, second, third


def shift_copy(axes, source, target, by, send_sem, recv_sem):
    size, index, at = axes["seq"]
    return pltpu.make_async_remote_copy(
        src_ref=source, dst_ref=target, send_sem=send_sem, recv_sem=recv_sem,
        device_id=at(lax.rem(index + by + size, size)), device_id_type=MESH,
    )


def padded(count, unit):
    return -(-count // unit) * unit


def piece_of(rows):
    return max(n for n in range(16, 513, 16) if rows % n == 0)


class Job:
    def __init__(self, src, dst, recv, recv_base, base, rows, order, axes, send_sems, recv_sems, own_sem):
        self.src, self.dst, self.recv = src, dst, recv
        self.send_sems, self.recv_sems = send_sems, recv_sems
        self.axes = [axes[name] for name in order]
        self.spans = [(base, rows)]
        self.slots = []
        for size, index, _ in self.axes:
            at, span = self.spans[-1]
            part = span // size
            self.spans.append((pl.multiple_of(at + index * part, 16), part))
            self.slots.append(recv_base)
            recv_base += (size - 1) * part
        self.stages = 2 * len(self.axes)
        self.end = base + rows
        own, part = self.spans[-1]
        self.result = recv.at[pl.ds(self.slots[-1], part)]
        self.keep = pltpu.make_async_copy(self.result, dst.at[pl.ds(own, part)], own_sem)

    def copies(self, stage):
        down = stage < len(self.axes)
        level = stage if down else self.stages - 1 - stage
        size, index, at = self.axes[level]
        base, _ = self.spans[level]
        own, part = self.spans[level + 1]
        result = []
        for k in range(1, size):
            partner = lax.rem(index + k, size)
            if down:
                if level == 0:
                    source = self.src.at[pl.ds(pl.multiple_of(base + partner * part, 16), part)]
                else:
                    held = self.slots[level - 1]
                    source = self.recv.at[pl.ds(pl.multiple_of(held + partner * part, 16), part)]
                target = self.recv.at[pl.ds(self.slots[level] + (k - 1) * part, part)]
            else:
                target = self.dst.at[pl.ds(own, part)]
                source = self.result if stage == len(self.axes) else target
            result.append(
                pltpu.make_async_remote_copy(
                    src_ref=source,
                    dst_ref=target,
                    send_sem=self.send_sems.at[stage, k - 1],
                    recv_sem=self.recv_sems.at[stage, k - 1],
                    device_id=at(partner),
                    device_id_type=MESH,
                )
            )
        return result

    def start(self, stage):
        for copy in self.copies(stage):
            copy.start()

    def move(self, stage):
        if stage > 0:
            self.finish(stage - 1)
        if stage < self.stages:
            self.start(stage)

    def finish(self, stage):
        for copy in self.copies(stage):
            copy.wait()
        if stage == len(self.axes):
            self.keep.wait()
        if stage >= len(self.axes):
            return
        size, index, _ = self.axes[stage]
        own, part = self.spans[stage + 1]
        slot = self.slots[stage]
        step = piece_of(part)

        @pl.loop(0, part // step)
        def _(i):
            def rows(start):
                return pl.ds(pl.multiple_of(start + i * step, 16), step)

            if stage == 0:
                total = self.src[rows(own), :].astype(F32)
            else:
                total = self.recv[rows(self.slots[stage - 1] + index * part), :].astype(F32)
            for k in range(size - 1):
                total = total + self.recv[rows(slot + k * part), :].astype(F32)
            self.recv[rows(slot), :] = total.astype(BF16)

        if stage == len(self.axes) - 1:
            self.keep.start()


class VectorJob:
    def __init__(self, total, recv, order, axes, send_sems, recv_sems):
        self.total, self.recv, self.send_sems, self.recv_sems = total, recv, send_sems, recv_sems
        self.axes = [axes[name] for name in order]
        self.slots = [sum(axis[0] for axis in self.axes[:i]) for i in range(len(self.axes))]

    def copies(self, stage):
        size, index, at = self.axes[stage]
        slot = self.slots[stage] + index
        return [
            pltpu.make_async_remote_copy(
                src_ref=self.recv.at[slot],
                dst_ref=self.recv.at[slot],
                send_sem=self.send_sems.at[stage, k - 1],
                recv_sem=self.recv_sems.at[stage, k - 1],
                device_id=at(lax.rem(index + k, size)),
                device_id_type=MESH,
            )
            for k in range(1, size)
        ]

    def start(self, stage):
        self.recv[self.slots[stage] + self.axes[stage][1]] = self.total[...]
        for copy in self.copies(stage):
            copy.start()

    def finish(self, stage):
        for copy in self.copies(stage):
            copy.wait()
        slot = self.slots[stage]
        total = self.recv[slot]
        for k in range(1, self.axes[stage][0]):
            total = total + self.recv[slot + k]
        self.total[...] = total


EARLY_JOBS = (9, 9, 9, 9)
LATE_JOBS = (3, 3, 3, 3, 3, 3, 2, 2)
MOST_JOBS = 8
ORDERS = (("core", "x", "y", "z"), ("core", "y", "x", "z"))
STAGES = 8


def jobs_of(sizes, src, dst, recv, axes, send_sems, recv_sems, own_sems):
    unit = 16 * lax.axis_size("dp") * lax.axis_size("seq")
    units = src.shape[0] // unit
    if sum(sizes) != units:
        sizes = [1] * units
    jobs = []
    base = 0
    for n, size in enumerate(sizes):
        rows = size * unit
        jobs.append(
            Job(
                src, dst, recv, base, base, rows, ORDERS[n % 2], axes, send_sems.at[n], recv_sems.at[n], own_sems.at[n]
            )
        )
        base += rows
    return jobs


def job_sems():
    return pltpu.SemaphoreType.DMA((JOBS, STAGES, max(axis_sizes()) - 1))


def pack_slabs(packed_ref, at, rows, first, value):
    count, width = value.shape
    for n in range(width // LANES):
        start = at + n * rows + first
        packed_ref[start : start + count, :] = value[:, n * LANES : (n + 1) * LANES].astype(BF16)


def enter_kernel(
    tok_ref, tail_ref, last_ref, gain_ref, wx_ref, wdt_in, weight_ref, bias_ref, dtb_ref, a_log_ref,
    normed_ref, xbc_ref, x_ref, bc_ref, dt_ref, sig_ref, added_ref, state_ref, logd_ref, xhalo_ref,
    product, spread, ext, state, suffix, prev, halo, xbc_send, xbc_halo, heads_ref, conv_ref, wdt_ref,
    halo_send, halo_recv, xbc_sems,
):
    step = pl.program_id(0)
    steps = pl.num_programs(0)
    inner = x_ref.shape[1]
    width = xbc_ref.shape[1]
    features = tok_ref.shape[2]
    axes = places()
    shift = shift_copy(axes, last_ref.at[0], halo, 1, halo_send, halo_recv)
    xbc_shift = shift_copy(axes, xbc_send, xbc_halo, 1, xbc_sems.at[0], xbc_sems.at[1])

    @pl.when(step == 0)
    def _():
        greet(axes, ("seq",))
        shift.start()
        set_spread(spread)
        set_rate(heads_ref, a_log_ref)
        heads_ref[DT_BIAS : DT_BIAS + 1, :] = head_row(dtb_ref[...])
        heads_ref[REAL : REAL + 1, :] = head_row(jnp.ones_like(dtb_ref))
        set_conv(conv_ref, weight_ref, bias_ref)
        set_step_weight(wdt_ref, wdt_in)
        state[...] = jnp.zeros_like(state)
        suffix[...] = jnp.zeros_like(suffix)

    @pl.when(step < steps - 1)
    def _():
        prev[...] = tail_ref[0]

    @pl.when(step == steps - 1)
    def _():
        shift.wait()
        prev[...] = jnp.where(axes["seq"][1] == 0, jnp.zeros_like(prev), halo[...])

    gain = gain_ref[...].reshape(1, -1)
    normed = normed_of(tok_ref[0], gain)
    both = jnp.concatenate([normed_of(prev[...], gain), normed], axis=0)
    normed_ref[...] = normed
    product[...] = dot(both, wx_ref[...])
    for n in range(width // LANES):
        lanes = slice(n * LANES, (n + 1) * LANES)
        part = product[:, lanes].astype(BF16)
        xbc_ref[:, lanes] = part[RIM:]
        ext[n] = part.astype(F32)

    @pl.when(step == 0)
    def _():
        xbc_send[...] = xbc_ref[BLOCK - RIM :, :]
        xbc_shift.start()

    real = heads_ref[REAL : REAL + 1, :]
    dt_raw = dot_t(normed, wdt_ref[...]) + heads_ref[DT_BIAS : DT_BIAS + 1, :]
    softplus = jnp.maximum(dt_raw, 0.0) + jnp.log1p(jnp.exp(-jnp.abs(dt_raw)))
    dt_low = (softplus * real).astype(BF16)
    dt_ref[...] = dt_low
    sig_ref[...] = sigmoid(dt_raw)

    def conv(lane, dst_ref, dst_lane):
        lanes = tile(lane)
        taps = [conv_ref[k : k + 1, lanes] for k in range(CONV)]
        bias = conv_ref[CONV : CONV + 1, lanes]
        for row in range(0, BLOCK, 64):
            total = bias
            for k in range(CONV):
                at = row + RIM - (CONV - 1) + k
                total = total + taps[k] * ext[lane, at : at + 64, :]
            dst_ref[row : row + 64, tile(dst_lane)] = (total * sigmoid(total)).astype(BF16)

    for lane in range(2):
        conv(inner // LANES + lane, bc_ref, lane)

    @pl.loop(0, inner // LANES)
    def _(lane):
        conv(lane, x_ref, lane)

    ones = lower_ones(SUB)
    factors = []
    finals = []
    for sub in range(SUBS):
        dt_sub = dt_low[sub * SUB : (sub + 1) * SUB]
        run = dot(ones, dt_sub) * heads_ref[RATE : RATE + 1, :]
        final = run[SUB - 1 : SUB]
        factors.append(parts(jnp.exp2(final - run) * dt_sub.astype(F32)))
        finals.append(parts(jnp.broadcast_to(final, (8, LANES))))
    b_flip = [flip(bc_ref[sub * SUB : (sub + 1) * SUB, :STATE]) for sub in range(SUBS)]
    product[:, :inner] = dot(jnp.concatenate(factors + finals, axis=0), spread[...])
    for sub in reversed(range(SUBS)):
        rows = slice(sub * SUB, (sub + 1) * SUB)
        at = SUBS * SUB + 8 * sub
        weighted = (product[rows, :inner] * x_ref[rows, :].astype(F32)).astype(BF16)
        added = dot(b_flip[sub], weighted)
        added_ref[sub] = added.astype(BF16)
        state[...] += jnp.exp2(suffix[0:1, :]) * added
        suffix[...] += product[at : at + 8, :inner]

    @pl.when(step == steps - 1)
    def _():
        state_ref[...] = state[...].astype(BF16)
        logd_ref[...] = suffix[...]
        xbc_shift.wait()
        xhalo_ref[...] = jnp.where(axes["seq"][1] == 0, jnp.zeros_like(xbc_halo), xbc_halo[...])


def middle_kernel(
    len_ref, tok_ref, cot_ref, normed_ref, x_ref, bc_ref, dt_ref, added_ref, state_ref, logd_ref,
    wz_ref, wo_ref, gain_ref, a_log_ref, skip_in,
    out_ref, gy_ref, gz_ref, starts_ref, rowdot_ref, adj_ref, pack_ref, ggain_ref, logds_ref, norm_t_ref,
    wide, spread, scan, state, prefix, skip, gate, go, o_all, gz_all, gb_all, norm_t, adj, ggain, pair_state, chip_state, chips, logds,
    heads_ref, gains_ref, slot_send, slot_recv, log_send, log_recv,
):
    step = pl.program_id(0)
    steps = pl.num_programs(0) // 2
    inner = x_ref.shape[1]
    features = tok_ref.shape[2]
    tok_rows = steps * BLOCK
    axes = places()
    count, me, _ = axes["seq"]
    core = axes["core"][1]
    y_count, y, _ = axes["y"]
    half, pair_copies, chip_copies, half_copies = two_level(
        axes, state_ref, pair_state, chip_state, chips, slot_send, slot_recv
    )
    pair_copies += state_copies(axes, logd_ref, logds, log_send, log_recv)
    ones = lower_ones(SUB)

    @pl.when(step == 0)
    def _():
        greet(axes, ("seq",))
        for copy in pair_copies:
            copy.start()
        logds[me] = logd_ref[...]
        set_spread(spread)
        set_rate(heads_ref, a_log_ref)
        heads_ref[SKIP : SKIP + 1, :] = head_row(skip_in[...])
        gains_ref[1:2, :] = gain_ref[...].reshape(1, -1)
        prefix[...] = jnp.zeros_like(prefix)
        adj[...] = jnp.zeros_like(adj)
        ggain[...] = jnp.zeros_like(ggain)
        for lanes in chunks(inner):
            skip[:, lanes] = dot(
                parts(jnp.broadcast_to(heads_ref[SKIP : SKIP + 1, :], (8, LANES))), spread[:, lanes]
            )

    @pl.when(step < steps)
    def _():
        row_i, col_i = grid2(SUB)
        causal = row_i >= col_i
        first_half = half_mask()
        for sub in range(SUBS):
            rows = slice(sub * SUB, (sub + 1) * SUB)
            dt_low = dt_ref[rows]
            meet = jnp.where(causal, dot_t(bc_ref[rows, STATE:], bc_ref[rows, :STATE]), 0.0)
            run = dot(ones, dt_low) * heads_ref[RATE : RATE + 1, :]
            run_t = run.T
            first_row = step * BLOCK + sub * SUB
            all_rows = pl.ds(pl.multiple_of(first_row, SUB), SUB)
            live = me * tok_rows + first_row + lax.broadcasted_iota(jnp.int32, (SUB, 1), 0) < len_ref[0]
            g_branch = jnp.where(live, cot_ref[0, rows, :], jnp.zeros((SUB, features), BF16))
            gb_all[all_rows, :] = g_branch
            normed = normed_ref[rows, :]
            norm_t[:, all_rows] = flip(normed)
            wide[:SUB, :] = dot(dt_low, spread[...])
            if sub == SUBS - 1:
                block_rows = tile(step, BLOCK)
                gate[block_rows, :] = dot(normed_ref[...], wz_ref[...])
                go[block_rows, :] = dot_t(gb_all[block_rows, :], wo_ref[...])
            for pair in range(inner // LANES):
                lanes = slice(pair * LANES, (pair + 1) * LANES)
                inflow = wide[:SUB, lanes] * x_ref[rows, lanes].astype(F32)
                scores = []
                for head in (2 * pair, 2 * pair + 1):
                    gap = jnp.minimum(run[:, head : head + 1] - run_t[head : head + 1, :], 0.0)
                    scores.append((jnp.exp2(gap) * meet).astype(BF16))
                scan[step, rows, lanes] = dot(
                    jnp.concatenate(scores, axis=1), pair_diag(inflow.astype(BF16), first_half)
                )

    @pl.when(step == 0)
    def _():
        for copy in pair_copies:
            copy.wait()
        mine, other = state_ref[:, half].astype(F32), pair_state[:, half].astype(F32)
        decay = jnp.exp2(logds[2 * y + 1, 0:1, half])
        chip_state[...] = jnp.where(core == 0, decay * mine + other, decay * other + mine).astype(BF16)
        for copy in chip_copies:
            copy.start()

    @pl.when(step == steps // 2)
    def _():
        for copy in chip_copies:
            copy.wait()
        for copy in half_copies:
            copy.start()

    @pl.when(step == steps)
    def _():
        for copy in half_copies:
            copy.wait()
        logds_ref[...] = logds[...]
        for lanes in chunks(inner):
            total = jnp.zeros((STATE, WIDE), F32)
            for chip in range(y_count):
                decay = jnp.exp2(logds[2 * chip, 0:1, lanes] + logds[2 * chip + 1, 0:1, lanes])
                total = jnp.where(chip < y, decay * total + chips[chip, :, lanes].astype(F32), total)
            decay = jnp.exp2(logds[2 * y, 0:1, lanes])
            state[:, lanes] = jnp.where(core == 1, decay * total + pair_state[:, lanes].astype(F32), total)

    @pl.when(step >= steps)
    def _():
        block = step - steps
        live = (
            me * tok_rows + block * BLOCK + lax.broadcasted_iota(jnp.int32, (BLOCK, 1), 0) < len_ref[0]
        )
        adj_factors = []
        for sub in range(SUBS):
            rows = slice(sub * SUB, (sub + 1) * SUB)
            c_out = bc_ref[rows, STATE:]
            run = dot(ones, dt_ref[rows]) * heads_ref[RATE : RATE + 1, :]
            final = run[SUB - 1 : SUB]
            factors = [parts(jnp.exp2(run)), parts(jnp.broadcast_to(jnp.exp2(final), (16, LANES)))]
            adj_factors.append(parts(jnp.exp2(run + prefix[0:1, :])))
            prefix[...] += final
            low = state[...].astype(BF16)
            starts_ref[sub] = low
            wide[...] = dot(jnp.concatenate(factors, axis=0), spread[...])
            scan[block, rows, :] += wide[:SUB, :] * dot(c_out, low)
            state[...] = wide[SUB : SUB + 1, :] * state[...] + added_ref[sub].astype(F32)
        base = pl.multiple_of(block * BLOCK, BLOCK)

        @pl.loop(0, BLOCK // 32, unroll=2)
        def _(chunk):
            rows = tile(chunk, 32)
            all_rows = pl.ds(pl.multiple_of(base + chunk * 32, 32), 32)
            square = jnp.zeros((32, LANES), F32)
            cross = jnp.zeros((32, LANES), F32)
            for lane in range(inner // LANES):
                lanes = slice(lane * LANES, (lane + 1) * LANES)
                y = (scan[block, rows, lanes] + skip[0:1, lanes] * x_ref[rows, lanes].astype(F32)).astype(BF16)
                o_all[all_rows, lanes] = y
                pre = gate[all_rows, lanes]
                gated = y.astype(F32) * (pre * sigmoid(pre))
                square += gated * gated
                cross += go[all_rows, lanes] * gains_ref[1:2, lanes] * gated
            rms = lax.rsqrt(jnp.sum(square, axis=-1, keepdims=True) * (1.0 / inner) + EPSILON)
            pull = jnp.sum(cross, axis=-1, keepdims=True) * (1.0 / inner) * rms * rms * rms
            rms = jnp.broadcast_to(rms, (32, LANES))
            pull = jnp.broadcast_to(pull, (32, LANES))
            for lane in range(inner // LANES):
                lanes = slice(lane * LANES, (lane + 1) * LANES)
                y = o_all[all_rows, lanes].astype(F32)
                pre = gate[all_rows, lanes]
                sig = sigmoid(pre)
                silu = pre * sig
                gated = y * silu
                gain = gains_ref[1:2, lanes]
                g_o = go[all_rows, lanes]
                unit = gated * rms
                o_all[all_rows, lanes] = (unit * gain).astype(BF16)
                ggain[:, lanes] += fold(g_o * unit)
                g_gated = rms * (g_o * gain) - pull * gated
                g_y = (g_gated * silu).astype(BF16)
                gy_ref[rows, lanes] = g_y
                g_z = (g_gated * y * (sig + silu * (1.0 - sig))).astype(BF16)
                gz_ref[rows, lanes] = g_z
                gz_all[all_rows, lanes] = g_z
                go[all_rows, lanes] = g_y.astype(F32) * scan[block, rows, lanes]

        branch = dot(o_all[tile(block, BLOCK), :], wo_ref[...])
        out_ref[0] = (tok_ref[0].astype(F32) + jnp.where(live, branch, 0.0)).astype(BF16)
        product = go[tile(block, BLOCK), :]
        high = product.astype(BF16)
        low = (product - high.astype(F32)).astype(BF16)
        head_sums = dot_t(jnp.concatenate([high, low], axis=0), spread[...])
        rowdot_ref[...] = head_sums[:BLOCK] + head_sums[BLOCK:]
        c_flip = jnp.concatenate([flip(bc_ref[sub * SUB : (sub + 1) * SUB, STATE:]) for sub in range(SUBS)], axis=1)
        factor = jnp.concatenate(adj_factors, axis=0)
        scaled = (dot(factor, spread[...]) * gy_ref[...].astype(F32)).astype(BF16)
        adj[...] += dot(c_flip, scaled)

    @pl.when(step == 2 * steps - 1)
    def _():
        norm_t_ref[...] = norm_t[...]
        adj_ref[...] = adj[...].astype(BF16)
        ggain_ref[...] = ggain[...]
        for lanes in chunks(inner):
            o_flip = flip(o_all[:, lanes])
            pack_slabs(pack_ref, 0, inner, lanes.start, dot(o_flip, gb_all[...]))
        for start in range(0, features, BLOCK):
            part = dot(norm_t[start : start + BLOCK, :], gz_all[...])
            pack_slabs(pack_ref, inner * features // LANES, features, start, part)
        used = 2 * inner * features // LANES
        if pack_ref.shape[0] > used:
            pack_ref[used:, :] = jnp.zeros((pack_ref.shape[0] - used, LANES), BF16)


def vector_rows(features, width, inner):
    counts = (features // LANES, CONV * width // LANES, width // LANES, inner // LANES, 1, 1, 1)
    starts = [sum(counts[:n]) for n in range(len(counts))]
    return starts, padded(sum(counts), 8)


def back_kernel(
    x_row, x_col, gy_row, gy_col, bc_ref, dt_ref, sig_ref, rowdot_ref, starts_ref, xbc_ref, xhalo_ref, xbc_rest, xhalo_rest, adj_ref,
    logds_ref, early_ref, ggain_ref, tok_ref, cot_ref, norm_t_in, gz_in, wz_in, wx_in, wdt_in,
    gain_ref, weight_ref, bias_ref, a_log_ref, skip_in,
    grad_ref, early_out, late_out, vec_out,
    spread, gather, ginf, factors, finals, c_flip, g_bc, x_ginf, column, d_final, skip, act, ext, gconv, gx_all, gdt_all,
    last, rim_send, rim_recv, gcw, gcb, gdtb, grate, gskip, gng, pair_adj, chip_adj, chips, early_recv, late_src, late_recv, vec, vec_recv,
    heads_ref, conv_ref, wdt_ref, norm_t, gz_ref, wz_ref, wx_ref,
    early_sems, late_sems, own_sems, vec_sems, slot_send, slot_recv, rim_sems, load_sems,
):
    step = pl.program_id(0)
    tok_rows, features = gx_all.shape[0], tok_ref.shape[2]
    inner = wz_ref.shape[1]
    width = wx_ref.shape[1]
    blocks = tok_rows // BLOCK
    subs = tok_rows // SUB
    pieces = inner // PIECE
    slab_rows = PIECE // LANES * features
    gn = ginf.at[:, pl.ds(0, features)]
    channel_step = blocks
    product_step = blocks + pieces
    norm_step = product_step + 1
    axes = places()
    count, me, _ = axes["seq"]
    core = axes["core"][1]
    y_count, y, _ = axes["y"]
    half, pair_copies, chip_copies, half_copies = two_level(
        axes, adj_ref, pair_adj, chip_adj, chips, slot_send, slot_recv
    )
    early = jobs_of(
        EARLY_JOBS, early_ref, early_out, early_recv, axes, early_sems.at[0], early_sems.at[1], own_sems.at[0]
    )
    late = jobs_of(LATE_JOBS, late_src, late_out, late_recv, axes, late_sems.at[0], late_sems.at[1], own_sems.at[1])
    vector = VectorJob(vec, vec_recv, ORDERS[0], axes, vec_sems.at[0], vec_sems.at[1])
    ones = lower_ones(SUB)
    row_i, col_i = grid2(SUB)
    later = row_i <= col_i

    loads = [
        pltpu.make_async_copy(source, target, load_sems.at[n])
        for n, (source, target) in enumerate(
            ((norm_t_in, norm_t), (gz_in, gz_ref), (wz_in, wz_ref), (wx_in, wx_ref))
        )
    ]

    channel_time = blocks * WITHIN_TIME
    product_time = channel_time + pieces * CHANNEL_TIME
    norm_time = product_time + PRODUCT_TIME
    end_time = norm_time + blocks * NORM_TIME
    moves = [
        (EARLY_PLAN[stage] + EARLY_SHIFT * (n // 2), job, stage)
        for n, job in enumerate(early)
        for stage in range(1, STAGES + 1)
    ]
    begins = []
    for job in late:
        piece = min((job.end - 1) // slab_rows, pieces)
        begins.append(piece + 1 + channel_step if piece < pieces else product_step)
        ready = channel_time + (piece + 1.3) * CHANNEL_TIME if piece < pieces else product_time + PRODUCT_TIME * 0.35
        moves += [(ready + LATE_PLAN[stage], job, stage) for stage in range(1, STAGES + 1)]
    moves.sort(key=lambda move: move[0])
    placed = []

    def advance(grid_step, since, until):
        due = [move for move in moves if since < move[0] <= until]
        placed.extend(due)
        if due:

            @pl.when(step == grid_step)
            def _():
                for _, job, stage in due:
                    job.move(stage)

    def advance_each(first, number, start, length, since, until):
        for n in range(number):
            base = start + n * length
            advance(first + n, base + since * length, base + until * length)

    @pl.when(step == 0)
    def _():
        greet(axes, ("seq", "x", "z"))
        for copy in pair_copies:
            copy.start()
        for job in early:
            job.start(0)
        for load in loads:
            load.start()
        set_spread(spread)
        for piece in range(inner // LANES):
            lanes = slice(piece * LANES, (piece + 1) * LANES)
            gather[lanes, :] = flip(spread[:, lanes])
        set_rate(heads_ref, a_log_ref)
        heads_ref[SKIP : SKIP + 1, :] = head_row(skip_in[...])
        set_conv(conv_ref, weight_ref, bias_ref)
        set_step_weight(wdt_ref, wdt_in)
        for lanes in chunks(inner):
            skip[:, lanes] = dot(
                parts(jnp.broadcast_to(heads_ref[SKIP : SKIP + 1, :], (8, LANES))), spread[:, lanes]
            )
        gconv[:, tok_rows:, :] = jnp.zeros((WIDE // LANES, 8, LANES), F32)
        for ref in (x_ginf, column, d_final, gcw, gcb, gdtb, grate, gskip, gng):
            ref[...] = jnp.zeros_like(ref)

    @pl.when(step < blocks)
    def _():
        first_half = half_mask()
        for sub in range(SUBS):
            rows = slice(sub * SUB, (sub + 1) * SUB)
            all_rows = pl.ds(pl.multiple_of(step * BLOCK + sub * SUB, SUB), SUB)
            number = step * SUBS + sub
            b_in, c_out = bc_ref[all_rows, :STATE], bc_ref[all_rows, STATE:]
            dt_low = dt_ref[all_rows, :]
            meet = jnp.where(later, dot_t(b_in, c_out), 0.0)
            run = dot(ones, dt_low) * heads_ref[RATE : RATE + 1, :]
            final = run[SUB - 1 : SUB]
            run_t = run.T
            factors[number] = jnp.concatenate(
                [dt_low, parts(jnp.exp2(final - run)), parts(jnp.exp2(run))], axis=0
            )
            finals[number] = parts(jnp.broadcast_to(jnp.exp2(final), (16, LANES)))
            c_flip[number] = flip(c_out)
            spread_dt = dot(dt_low, spread[...])
            g_meet = jnp.zeros((SUB, SUB), F32)
            for pair in range(inner // LANES):
                lanes = slice(pair * LANES, (pair + 1) * LANES)
                inflow = spread_dt[:, lanes] * x_row[rows, lanes].astype(F32)
                g_diag = pair_diag(gy_row[rows, lanes], first_half)
                g_scores = dot_t(inflow.astype(BF16), g_diag)
                scores = []
                for half, head in enumerate((2 * pair, 2 * pair + 1)):
                    decay = jnp.exp2(jnp.minimum(run_t[head : head + 1, :] - run[:, head : head + 1], 0.0))
                    scores.append((decay * meet).astype(BF16))
                    g_meet += decay * g_scores[:, half * SUB : (half + 1) * SUB]
                ginf[all_rows, lanes] = dot(jnp.concatenate(scores, axis=1), g_diag)
                if pair == inner // LANES // 2 - 1:
                    advance_each(0, blocks, 0.0, WITHIN_TIME, sub / SUBS, (sub + 0.5) / SUBS)
            g_meet = jnp.where(later, g_meet, 0.0).astype(BF16)
            g_bc[all_rows, :STATE] = dot(g_meet, c_out)
            g_bc[all_rows, STATE:] = t_dot(g_meet, b_in)
            advance_each(0, blocks, 0.0, WITHIN_TIME, (sub + 0.5) / SUBS, (sub + 1) / SUBS)

    @pl.when(step == 0)
    def _():
        for copy in pair_copies:
            copy.wait()
        mine, other = adj_ref[:, half].astype(F32), pair_adj[:, half].astype(F32)
        decay = jnp.exp2(logds_ref[2 * y, 0:1, half])
        chip_adj[...] = jnp.where(core == 0, mine + decay * other, other + decay * mine).astype(BF16)
        for copy in chip_copies:
            copy.start()

    @pl.when(step == blocks // 2)
    def _():
        for copy in chip_copies:
            copy.wait()
        for copy in half_copies:
            copy.start()

    @pl.when(step == channel_step)
    def _():
        for copy in half_copies:
            copy.wait()
        for load in loads:
            load.wait()

    def rim_copy(slot):
        return shift_copy(axes, rim_send.at[slot], rim_recv.at[slot], -1, rim_sems.at[0, slot], rim_sems.at[1, slot])

    def conv_back(slot, source, xbc, halo, at):
        for n in range(WIDE // LANES):
            lanes = slice(at + n * LANES, at + (n + 1) * LANES)
            ext[n, 0:RIM, :] = halo[:, lanes].astype(F32)
            ext[n, RIM:, :] = xbc[:, lanes].astype(F32)

        @pl.loop(0, WIDE // LANES)
        def _(n):
            lanes = tile(slot * (WIDE // LANES) + n)
            from_lanes = tile(at // LANES + n)
            taps = [conv_ref[k : k + 1, lanes] for k in range(CONV)]
            bias = conv_ref[CONV : CONV + 1, lanes]
            sums = [jnp.zeros((8, LANES), F32) for _ in range(CONV + 1)]
            for row in range(0, tok_rows, 64):
                start = row + RIM - (CONV - 1)
                shifted = [ext[n, start + k : start + k + 64, :] for k in range(CONV)]
                total = bias
                for k in range(CONV):
                    total = total + taps[k] * shifted[k]
                sig = sigmoid(total)
                g_act = source[row : row + 64, from_lanes].astype(F32)
                g_conv = g_act * (sig * (1.0 + total * (1.0 - sig)))
                gconv[n, row : row + 64, :] = g_conv
                for k in range(CONV):
                    sums[k] += fold(g_conv * shifted[k])
                sums[CONV] += fold(g_conv)
            for k in range(CONV):
                gcw[k, :, lanes] += sums[k]
            gcb[:, lanes] += sums[CONV]
            for row in range(0, tok_rows, 64):
                total = taps[CONV - 1] * gconv[n, row : row + 64, :]
                for k in range(CONV - 1):
                    start = row + CONV - 1 - k
                    total = total + taps[k] * gconv[n, start : start + 64, :]
                gx_all[row : row + 64, lanes] = total.astype(BF16)
            last[slot, :, tile(n)] = total[64 - RIM :]

        rim_send[slot] = gconv[:, 0:8, :]
        rim_copy(slot).start()

    def finish_slot(slot):
        rim_copy(slot).wait()
        row = lax.broadcasted_iota(jnp.int32, (8, LANES), 0)
        for n in range(WIDE // LANES):
            at = tile(slot * (WIDE // LANES) + n)
            rim = jnp.where(me == count - 1, jnp.zeros((8, LANES), F32), rim_recv[slot, n])
            fix = jnp.zeros((8, LANES), F32)
            for k in range(CONV - 1):
                moved = pltpu.roll(rim, 8 - CONV + 1 + k, 0)
                fix += jnp.where(row >= 8 - CONV + 1 + k, conv_ref[k : k + 1, at] * moved, 0.0)
            old = last[slot, :, n * LANES : (n + 1) * LANES]
            gx_all[tok_rows - RIM :, at] = jnp.concatenate([old[0:8], old[8:] + fix], axis=0).astype(BF16)

    def weight_gradient(piece, size):
        for m in range(features // BLOCK):
            part = dot(norm_t[m * BLOCK : (m + 1) * BLOCK, :], gx_all[:, pl.ds(pl.multiple_of(piece * PIECE, PIECE), size)])
            for n in range(size // LANES):
                at = pl.multiple_of(piece * slab_rows + n * features + m * BLOCK, 16)
                late_src[pl.ds(at, BLOCK), :] = part[:, n * LANES : (n + 1) * LANES].astype(BF16)

    def begin_late(last_piece):
        for job, begin in zip(late, begins):
            if ((job.end - 1) // slab_rows == pieces - 1) == last_piece and (job.end - 1) // slab_rows < pieces:

                @pl.when(step == begin)
                def _():
                    job.start(0)

    def finish_piece(piece, last_piece):
        for n in range(PIECE // WIDE):
            finish_slot(piece * (PIECE // WIDE) + n)
        weight_gradient(piece, PIECE)
        begin_late(last_piece)

    @pl.when((step >= channel_step) & (step < product_step))
    def _():
        piece = step - channel_step
        lanes = tile(piece, PIECE)
        spread_p = spread[:, lanes]
        gather_p = gather[lanes, :]
        skip_p = skip[0:1, lanes]
        after = jnp.zeros((STATE, PIECE), F32)
        for chip in reversed(range(y_count)):
            decay = jnp.exp2(logds_ref[2 * chip, 0:1, lanes] + logds_ref[2 * chip + 1, 0:1, lanes])
            after = jnp.where(chip > y, decay * after + chips[chip, :, lanes].astype(F32), after)
        decay = jnp.exp2(logds_ref[2 * y + 1, 0:1, lanes])
        after = jnp.where(core == 0, decay * after + pair_adj[:, lanes].astype(F32), after)
        skipped = [jnp.zeros((8, LANES), F32) for _ in range(PIECE // LANES)]
        for sub in reversed(range(subs)):
            rows = slice(sub * SUB, (sub + 1) * SUB)
            wide = dot(jnp.concatenate([factors[sub], finals[sub]], axis=0), spread_p)
            dt_e, to_end, from_start = wide[:SUB], wide[SUB : 2 * SUB], wide[2 * SUB : 3 * SUB]
            kept = wide[3 * SUB : 3 * SUB + 1]
            after_low = after.astype(BF16)
            start_low = starts_ref[sub]
            from_b = dot(bc_ref[rows, :STATE], after_low)
            operands = [[], [], [], [], []]
            block_sums = []
            for n in range(PIECE // LANES):
                at = slice(n * LANES, (n + 1) * LANES)
                columns = [[], [], [], [], []]
                block_sum = jnp.zeros((8, LANES), F32)
                skip_sum = jnp.zeros((8, LANES), F32)
                for row in range(0, SUB, 32):
                    here = slice(row, row + 32)
                    there = slice(sub * SUB + row, sub * SUB + row + 32)
                    x = x_col[there, at].astype(F32)
                    g_y = gy_col[there, at].astype(F32)
                    inflow = dt_e[here, at] * x
                    inflow_low = inflow.astype(BF16).astype(F32)
                    from_after = to_end[here, at] * from_b[here, at]
                    g_inflow = ginf[there, tile(piece * (PIECE // LANES) + n)] + from_after
                    act[there, at] = (dt_e[here, at] * g_inflow + skip_p[:, at] * g_y).astype(BF16)
                    product = inflow_low * g_inflow
                    high = product.astype(BF16)
                    columns[0].append((x * g_inflow).astype(BF16))
                    columns[1].append(high)
                    columns[2].append((product - high.astype(F32)).astype(BF16))
                    columns[3].append((from_start[here, at] * g_y).astype(BF16))
                    columns[4].append((to_end[here, at] * inflow).astype(BF16))
                    block_sum += fold(inflow_low * from_after)
                    skip_sum += fold(g_y * x)
                for operand, column_parts in zip(operands, columns):
                    operand.append(jnp.concatenate(column_parts, axis=0))
                block_sums.append(block_sum)
                skipped[n] += skip_sum
            x_g, high, low, scaled, weighted = [jnp.concatenate(operand, axis=1) for operand in operands]
            block_sum = jnp.concatenate(block_sums, axis=1) + kept * fold(
                start_low.astype(F32) * after_low.astype(F32)
            )
            sum_high = block_sum.astype(BF16).astype(F32)
            both = jnp.concatenate([sum_high, block_sum - sum_high], axis=0).astype(BF16)
            head_sums = dot(jnp.concatenate([x_g, high, low, both], axis=0), gather_p)
            x_ginf[rows, :] += head_sums[:SUB]
            column[rows, :] += head_sums[SUB : 2 * SUB] + head_sums[2 * SUB : 3 * SUB]
            d_final[sub] += head_sums[3 * SUB : 3 * SUB + 8] + head_sums[3 * SUB + 8 :]
            g_bc[rows, :STATE] += dot_t(weighted, after_low)
            g_bc[rows, STATE:] += dot_t(scaled, start_low)
            after = kept * after + dot(c_flip[sub], scaled)
            if sub == subs - 3:

                @pl.when(step > channel_step)
                def _():
                    finish_piece(piece - 1, False)

            done = (subs - sub) / subs * 0.7
            advance_each(channel_step, pieces, channel_time, CHANNEL_TIME, done - 0.7 / subs, done)
        gskip[:, lanes] += jnp.concatenate(skipped, axis=1)
        for n in range(PIECE // WIDE):
            conv_back(piece * (PIECE // WIDE) + n, act, xbc_ref, xhalo_ref, n * WIDE)
            since = 0.7 + 0.3 * n / (PIECE // WIDE)
            advance_each(
                channel_step, pieces, channel_time, CHANNEL_TIME, since, since + 0.3 / (PIECE // WIDE) + 1e-6
            )

    @pl.when(step == product_step)
    def _():
        conv_back(inner // WIDE, g_bc, xbc_rest, xhalo_rest, 0)
        finish_piece(pieces - 1, True)
        upper = jnp.where(later, 1.0, 0.0).astype(BF16)
        rate = heads_ref[RATE : RATE + 1, :] * (1.0 / LOG2E)
        rest = jnp.concatenate(
            [rowdot_ref[sub * SUB : (sub + 1) * SUB, :] - column[sub * SUB : (sub + 1) * SUB, :] for sub in range(subs)],
            axis=1,
        )
        sums = jnp.zeros_like(rest)
        for _ in range(3):
            part = rest.astype(BF16)
            sums += dot(upper, part)
            rest = rest - part.astype(F32)
        for sub in range(subs):
            rows = slice(sub * SUB, (sub + 1) * SUB)
            dt_f = dt_ref[rows, :].astype(F32)
            d_log = sums[:, sub * LANES : (sub + 1) * LANES]
            d_log = d_log + jnp.sum(d_final[sub], axis=0, keepdims=True)
            g_dt = (x_ginf[rows, :] + rate * d_log).astype(BF16).astype(F32)
            g_pre = g_dt * sig_ref[rows, :]
            gdt_all[rows, :] = g_pre.astype(BF16)
            gdtb[...] += fold(g_pre)
            grate[...] += fold(dt_f * d_log)
        advance(product_step, product_time, product_time + 0.2 * PRODUCT_TIME)
        finish_slot(inner // WIDE)
        weight_gradient(pieces, WIDE)
        at = width // LANES * features
        pack_slabs(late_src, at, 32, 0, dot_t(flip(gdt_all[...])[:32], norm_t[...]))
        used = at + 32 * features // LANES
        if late_src.shape[0] > used:
            late_src[used:, :] = jnp.zeros((late_src.shape[0] - used, LANES), BF16)
        for job in late:
            if (job.end - 1) // slab_rows >= pieces:
                job.start(0)
        for m in range(blocks):
            rows = slice(m * BLOCK, (m + 1) * BLOCK)
            gn[rows, :] = (
                dot_t(gz_ref[rows, :], wz_ref[...])
                + dot_t(gx_all[rows, :], wx_ref[...])
                + dot(gdt_all[rows, :], wdt_ref[...])
            )
            since = 0.2 if m == 0 else 0.4 + 0.6 * m / blocks
            until = 0.4 + 0.6 * (m + 1) / blocks
            advance(
                product_step, product_time + since * PRODUCT_TIME,
                product_time + until * PRODUCT_TIME if m < blocks - 1 else norm_time,
            )

    @pl.when(step >= norm_step)
    def _():
        block = step - norm_step
        rows = tile(block, BLOCK)
        g_normed = gn[rows, :]
        residual, rms = norm_rows(tok_ref[0])
        unit = residual * rms
        gng[...] += fold(g_normed * unit)
        h = g_normed * gain_ref[...].reshape(1, -1)
        pull = jnp.sum(h * unit, axis=-1, keepdims=True) * (1.0 / features)
        grad_ref[0] = (cot_ref[0].astype(F32) + rms * (h - unit * pull)).astype(BF16)
        advance_each(norm_step, blocks, norm_time, NORM_TIME, 0.0, 1.0)

    @pl.when(step == norm_step + blocks - 1)
    def _():
        starts, _ = vector_rows(features, width, inner)

        def put(row, ref):
            value = ref if ref.shape[0] == 1 else jnp.sum(ref, axis=0, keepdims=True)
            for n in range(value.shape[1] // LANES):
                vec[row + n : row + n + 1, :] = value[:, n * LANES : (n + 1) * LANES]

        vec[...] = jnp.zeros_like(vec)
        put(starts[0], gng[...])
        for k in range(CONV):
            put(starts[1] + k * width // LANES, gcw[k])
        put(starts[2], gcb[...])
        put(starts[3], ggain_ref[...])
        put(starts[4], gdtb[...])
        put(starts[5], grate[...] * (heads_ref[RATE : RATE + 1, :] * (1.0 / LOG2E)))
        put(starts[6], split_dot_t(gskip[...], spread[...]))
        vector.start(0)
        rest = [move for move in moves if move[0] > end_time]
        assert len(placed) + len(rest) == len(moves)
        for n, (_, job, stage) in enumerate(rest):
            job.move(stage)
            level, turn = divmod(n + 1, max(1, len(rest) // 5))
            if turn == 0 and level <= 4:
                vector.finish(level - 1)
                if level < 4:
                    vector.start(level)
        vec_out[...] = vec[...]


WITHIN_TIME = 5.0
CHANNEL_TIME = 12.0
PRODUCT_TIME = 14.0
NORM_TIME = 1.2
EARLY_PLAN = (0, 7, 19, 28, 40, 51, 60, 72, 79)
EARLY_SHIFT = 8
LATE_PLAN = (0, 4, 9, 13, 18, 23, 27, 32, 36)


def unpack_kernel(
    wo_ref, wz_ref, wx_ref, wdt_ref, vec_ref, out_in, grad_in,
    out_ref, grad_ref, gwo_ref, gwz_ref, gwx_ref, gwdt_ref, gng_ref, gcw_ref, gcb_ref, gdtb_ref, ga_ref, gskip_ref, ggain_ref,
):
    def slabs(source, target):
        rows = target.shape[0]
        for n in range(target.shape[1] // LANES):
            target[:, n * LANES : (n + 1) * LANES] = source[n * rows : (n + 1) * rows, :].astype(F32)

    out_ref[...] = out_in[...]
    grad_ref[...] = grad_in[...]
    slabs(wo_ref, gwo_ref)
    slabs(wz_ref, gwz_ref)
    slabs(wx_ref, gwx_ref)

    @pl.when(pl.program_id(0) == 0)
    def _():
        heads, features = gwdt_ref.shape
        width = gcb_ref.shape[0]
        at, _ = vector_rows(features, width, ggain_ref.shape[0])
        for n in range(features // LANES):
            gwdt_ref[:, n * LANES : (n + 1) * LANES] = wdt_ref[n * 32 : n * 32 + heads, :].astype(F32)

        def rows(start, size):
            return jnp.concatenate([vec_ref[start + n : start + n + 1, :] for n in range(size // LANES)], axis=1)

        gng_ref[...] = rows(at[0], features).reshape(-1)
        for k in range(CONV):
            gcw_ref[k : k + 1, :] = rows(at[1] + k * width // LANES, width)
        gcb_ref[...] = rows(at[2], width).reshape(-1)
        ggain_ref[...] = rows(at[3], ggain_ref.shape[0]).reshape(-1)
        for n, ref in enumerate((gdtb_ref, ga_ref, gskip_ref)):
            ref[...] = vec_ref[at[4 + n] : at[4 + n] + 1, :][0, :heads]


def unpack(early, late, vec, out, grad, inner, width, features, heads):
    sds = jax.ShapeDtypeStruct
    grid = width // WIDE
    last = inner // WIDE - 1
    first = inner * features // LANES // (2 * features)
    stop = width // LANES * features
    rest = 32 * features // LANES
    passed = pl.BlockSpec((1, BLOCK, features), lambda i: (0, jnp.minimum(i, out.shape[1] // BLOCK - 1), 0))
    vectors = [(heads, features), (features,), (CONV, width), (width,), (heads,), (heads,), (heads,), (inner,)]
    return pl.pallas_call(
        unpack_kernel,
        grid=(grid,),
        in_specs=[
            pl.BlockSpec((inner, LANES), lambda i: (jnp.minimum(i, features // LANES - 1), 0)),
            pl.BlockSpec((2 * features, LANES), lambda i: (first + jnp.minimum(i, last), 0)),
            pl.BlockSpec((2 * features, LANES), lambda i: (i, 0)),
            pl.BlockSpec((rest, LANES), lambda i: (stop // rest, 0)),
            whole(vec.shape), passed, passed,
        ],
        out_specs=[
            passed, passed,
            pl.BlockSpec((inner, LANES), lambda i: (0, jnp.minimum(i, features // LANES - 1))),
            pl.BlockSpec((features, WIDE), lambda i: (0, jnp.minimum(i, last))),
            pl.BlockSpec((features, WIDE), lambda i: (0, i)),
            *[whole(shape) for shape in vectors],
        ],
        out_shape=[
            sds(out.shape, BF16), sds(grad.shape, BF16),
            sds((inner, features), F32), sds((features, inner), F32), sds((features, width), F32),
            *[sds(shape, F32) for shape in vectors],
        ],
        compiler_params=pltpu.CompilerParams(vmem_limit_bytes=VMEM_LIMIT),
        name="unpack",
    )(early, early, late, late, vec, out, grad)


def whole(shape):
    return pl.BlockSpec(shape, lambda i: (0,) * len(shape), pipeline_mode=pl.Buffered(1))


def params(collective_id):
    return pltpu.CompilerParams(
        vmem_limit_bytes=VMEM_LIMIT, dimension_semantics=("arbitrary",), collective_id=collective_id, has_side_effects=True
    )


def local(
    tokens, lengths, cotangent, norm_gain, w_z, w_xbc, w_dt, conv_weight, conv_bias, dt_bias, a_log, d_skip, gate_gain, w_out
):
    tok_rows, features = tokens.shape[1:]
    inner = w_z.shape[1]
    width = w_xbc.shape[1]
    heads = a_log.shape[0]
    steps = tok_rows // BLOCK
    seq_count = lax.axis_size("seq")
    devices = lax.axis_size("dp") * seq_count
    sds = jax.ShapeDtypeStruct
    dma = pltpu.SemaphoreType.DMA

    head_scratch = [pltpu.VMEM((8, LANES), F32)]

    def rows3(n, at, single=False):
        return pl.BlockSpec((1, BLOCK, n), lambda i: (0, at(i), 0), pipeline_mode=pl.Buffered(1 if single else 2))

    def rows2(n, at, single=False):
        return pl.BlockSpec((BLOCK, n), lambda i: (at(i), 0), pipeline_mode=pl.Buffered(1 if single else 2))

    def tail_at(block):
        return jnp.maximum(block * (BLOCK // RIM) - 1, 0)

    def back(i):
        return steps - 1 - i

    normed, xbc, x, bc, dt, sig, added, state, logd, xbc_halo = pl.pallas_call(
        enter_kernel,
        grid=(steps,),
        in_specs=[
            rows3(features, back),
            pl.BlockSpec((1, RIM, features), lambda i: (0, tail_at(back(i)), 0)),
            pl.BlockSpec((1, RIM, features), lambda i: (0, tok_rows // RIM - 1, 0), pipeline_mode=pl.Buffered(1)),
            whole((features,)), whole((features, width)), whole((heads, features)), whole((CONV, width)), whole((width,)),
            whole((heads,)), whole((heads,)),
        ],
        out_specs=[
            rows2(features, back), rows2(width, back), rows2(inner, back), rows2(2 * STATE, back), rows2(LANES, back),
            rows2(LANES, back), pl.BlockSpec((SUBS, STATE, inner), lambda i: (back(i), 0, 0)),
            whole((STATE, inner)), whole((8, inner)), whole((RIM, width)),
        ],
        out_shape=[
            sds((tok_rows, features), BF16), sds((tok_rows, width), BF16), sds((tok_rows, inner), BF16),
            sds((tok_rows, 2 * STATE), BF16), sds((tok_rows, LANES), BF16), sds((tok_rows, LANES), F32),
            sds((tok_rows // SUB, STATE, inner), BF16), sds((STATE, inner), BF16), sds((8, inner), F32),
            sds((RIM, width), BF16),
        ],
        scratch_shapes=[
            pltpu.VMEM((BLOCK + RIM, width), F32),
            pltpu.VMEM((LANES, inner), BF16), pltpu.VMEM((width // LANES, BLOCK + RIM, LANES), F32),
            pltpu.VMEM((STATE, inner), F32), pltpu.VMEM((8, inner), F32), pltpu.VMEM((RIM, features), BF16),
            pltpu.VMEM((RIM, features), BF16), pltpu.VMEM((RIM, width), BF16), pltpu.VMEM((RIM, width), BF16), *head_scratch, pltpu.VMEM((8, width), F32),
            pltpu.VMEM((LANES, features), BF16), dma, dma, dma((2,)),
        ],
        compiler_params=params(0),
        name="enter",
    )(tokens, tokens, tokens, norm_gain, w_xbc, w_dt.T, conv_weight, conv_bias, dt_bias, a_log)

    count = seq_count - 1
    early_rows = padded(2 * inner * features // LANES, 16 * devices)
    late_rows = padded((width + 32) * features // LANES, 16 * devices)

    def either(i):
        return lax.rem(i, steps)

    def second(i):
        return jnp.maximum(i - steps, 0)

    out, g_y, g_z, starts, rowdot, adj, early, g_gain, logds, norm_t = pl.pallas_call(
        middle_kernel,
        grid=(2 * steps,),
        in_specs=[
            pl.BlockSpec(memory_space=pltpu.SMEM),
            rows3(features, second), rows3(features, either), rows2(features, either), rows2(inner, either),
            rows2(2 * STATE, either), rows2(LANES, either),
            pl.BlockSpec((SUBS, STATE, inner), lambda i: (second(i), 0, 0)), whole((STATE, inner)), whole((8, inner)),
            whole((features, inner)), whole((inner, features)), whole((inner,)), whole((heads,)), whole((heads,)),
        ],
        out_specs=[
            rows3(features, second), rows2(inner, second), rows2(inner, second),
            pl.BlockSpec((SUBS, STATE, inner), lambda i: (second(i), 0, 0)),
            rows2(LANES, second), whole((STATE, inner)), whole((early_rows, LANES)), whole((8, inner)),
            whole((seq_count, 8, inner)), whole((features, tok_rows)),
        ],
        out_shape=[
            sds((1, tok_rows, features), BF16), sds((tok_rows, inner), BF16), sds((tok_rows, inner), BF16),
            sds((tok_rows // SUB, STATE, inner), BF16), sds((tok_rows, LANES), F32),
            sds((STATE, inner), BF16), sds((early_rows, LANES), BF16), sds((8, inner), F32),
            sds((seq_count, 8, inner), F32), sds((features, tok_rows), BF16),
        ],
        scratch_shapes=[
            pltpu.VMEM((SUB + 16, inner), F32),
            pltpu.VMEM((LANES, inner), BF16), pltpu.VMEM((steps, BLOCK, inner), F32), pltpu.VMEM((STATE, inner), F32),
            pltpu.VMEM((8, LANES), F32), pltpu.VMEM((8, inner), F32), pltpu.VMEM((tok_rows, inner), F32),
            pltpu.VMEM((tok_rows, inner), F32), pltpu.VMEM((tok_rows, inner), BF16), pltpu.VMEM((tok_rows, inner), BF16),
            pltpu.VMEM((tok_rows, features), BF16), pltpu.VMEM((features, tok_rows), BF16),
            pltpu.VMEM((STATE, inner), F32), pltpu.VMEM((8, inner), F32),
            pltpu.VMEM((STATE, inner), BF16), pltpu.VMEM((STATE, inner // 2), BF16),
            pltpu.VMEM((seq_count // 2, STATE, inner), BF16), pltpu.VMEM((seq_count, 8, inner), F32),
            *head_scratch, pltpu.VMEM((8, inner), F32), dma((seq_count,)), dma((seq_count,)), dma((count,)), dma((count,)),
        ],
        compiler_params=params(1),
        name="middle",
    )(lengths, tokens, cotangent, normed, x, bc, dt, added, state, logd, w_z, w_out, gate_gain, a_log, d_skip)

    pieces = inner // PIECE
    norm_step = steps + pieces + 1

    def first(i):
        return jnp.minimum(i, steps - 1)

    def column(rows, most):
        return pl.BlockSpec((rows, PIECE), lambda i: (0, jnp.clip(i - steps, 0, most)))

    def rest(rows):
        return pl.BlockSpec((rows, WIDE), lambda i: (0, inner // WIDE), pipeline_mode=pl.Buffered(1))

    def final(i):
        return jnp.clip(i - norm_step, 0, steps - 1)

    _, vec_rows = vector_rows(features, width, inner)
    sizes = axis_sizes()
    reach = max(sizes) - 1
    tiles = WIDE // LANES
    grad, early, late, vec = pl.pallas_call(
        back_kernel,
        grid=(norm_step + steps,),
        in_specs=[
            rows2(inner, first, True), column(tok_rows, pieces - 1), rows2(inner, first, True), column(tok_rows, pieces - 1),
            whole((tok_rows, 2 * STATE)), whole((tok_rows, LANES)), whole((tok_rows, LANES)), whole((tok_rows, LANES)),
            pl.BlockSpec((tok_rows // SUB, STATE, PIECE), lambda i: (0, 0, jnp.clip(i - steps, 0, pieces - 1))),
            column(tok_rows, pieces - 1), column(RIM, pieces - 1), rest(tok_rows), rest(RIM),
            whole((STATE, inner)), whole((seq_count, 8, inner)), whole((early_rows, LANES)), whole((8, inner)),
            rows3(features, final, True), rows3(features, final, True), *[pl.BlockSpec(memory_space=pl.ANY)] * 4,
            whole((heads, features)), whole((features,)),
            whole((CONV, width)), whole((width,)), whole((heads,)), whole((heads,)),
        ],
        out_specs=[
            rows3(features, final), pl.BlockSpec(memory_space=pl.ANY), pl.BlockSpec(memory_space=pl.ANY),
            whole((vec_rows, LANES)),
        ],
        out_shape=[
            sds((1, tok_rows, features), BF16), sds((early_rows, LANES), BF16), sds((late_rows, LANES), BF16),
            sds((vec_rows, LANES), F32),
        ],
        scratch_shapes=[
            pltpu.VMEM((LANES, inner), BF16), pltpu.VMEM((inner, LANES), BF16), pltpu.VMEM((tok_rows, inner), F32),
            pltpu.VMEM((tok_rows // SUB, 3 * SUB, LANES), BF16), pltpu.VMEM((tok_rows // SUB, 16, LANES), BF16),
            pltpu.VMEM((tok_rows // SUB, STATE, SUB), BF16), pltpu.VMEM((tok_rows, 2 * STATE), F32),
            pltpu.VMEM((tok_rows, LANES), F32), pltpu.VMEM((tok_rows, LANES), F32),
            pltpu.VMEM((tok_rows // SUB, 8, LANES), F32), pltpu.VMEM((8, inner), F32),
            pltpu.VMEM((tok_rows, PIECE), BF16), pltpu.VMEM((tiles, tok_rows + RIM, LANES), F32),
            pltpu.VMEM((tiles, tok_rows + 8, LANES), F32), pltpu.VMEM((tok_rows, width), BF16),
            pltpu.VMEM((tok_rows, LANES), BF16), pltpu.VMEM((width // WIDE, RIM, WIDE), F32),
            pltpu.VMEM((width // WIDE, tiles, 8, LANES), F32), pltpu.VMEM((width // WIDE, tiles, 8, LANES), F32),
            pltpu.VMEM((CONV, 8, width), F32), pltpu.VMEM((8, width), F32), pltpu.VMEM((8, LANES), F32),
            pltpu.VMEM((8, LANES), F32), pltpu.VMEM((8, inner), F32), pltpu.VMEM((8, features), F32),
            pltpu.VMEM((STATE, inner), BF16), pltpu.VMEM((STATE, inner // 2), BF16),
            pltpu.VMEM((seq_count // 2, STATE, inner), BF16), pltpu.VMEM((early_rows, LANES), BF16),
            pltpu.VMEM((late_rows, LANES), BF16), pltpu.VMEM((late_rows, LANES), BF16),
            pltpu.VMEM((vec_rows, LANES), F32), pltpu.VMEM((sum(sizes), vec_rows, LANES), F32),
            *head_scratch, pltpu.VMEM((8, width), F32), pltpu.VMEM((LANES, features), BF16),
            pltpu.VMEM((features, tok_rows), BF16), pltpu.VMEM((tok_rows, inner), BF16),
            pltpu.VMEM((features, inner), BF16), pltpu.VMEM((features, width), BF16),
            dma((2, MOST_JOBS, STAGES, reach)), dma((2, MOST_JOBS, STAGES, reach)), dma((2, MOST_JOBS)),
            dma((2, 4, reach)), dma((seq_count,)), dma((seq_count,)), dma((2, width // WIDE)), dma((4,)),
        ],
        compiler_params=params(2),
        name="back",
    )(
        x, x, g_y, g_y, bc, dt, sig, rowdot, starts, xbc, xbc_halo, xbc, xbc_halo, adj, logds, early, g_gain,
        tokens, cotangent, norm_t, g_z, w_z, w_xbc, w_dt.T, norm_gain, conv_weight, conv_bias, a_log, d_skip,
    )

    out, grad, g_wo, g_wz, g_wx, g_wdt, g_ng, g_cw, g_cb, g_dtb, g_a, g_skip, g_gain = unpack(
        early, late, vec, out, grad, inner, width, features, heads
    )
    return out, grad, g_ng, g_wz, g_wx, g_wdt.T, g_cw, g_cb, g_dtb, g_a, g_skip, g_gain, g_wo


def solution(mesh):
    rows = P("dp", "seq", None)
    return jax.shard_map(
        local,
        mesh=mesh,
        in_specs=(rows, P("dp"), rows) + (P(),) * 11,
        out_specs=(rows, rows) + (P(),) * 11,
        check_vma=False,
    )
```
